256 devices in a mesh: pat: 8 (over x, core), slab: 32 (over y, z).
Axes of the slice: x: 4, y: 4, z: 8, core: 2. Of those that a mesh axis runs over, the one named last changes fastest.
Arguments:
- features: bfloat16 [8, 64, 192, 384], P('pat', None, 'slab'), may hold values from -50 to 50
- cotangent: bfloat16 [8, 64, 192, 384], P('pat', None, 'slab'), may hold values from -50 to 50
- weights: float32 [2, 64, 1728], replicated, may hold values from -0.15625 to 0.15625
- prev_state: float32 [2, 64, 1728], replicated, may hold values from -6 to 6
- tree_noise: float32 [2, 64, 1728], replicated, may hold values from -6 to 6
Outputs:
- state_next: float32 [2, 64, 1728], replicated
- weights_next: float32 [2, 64, 1728], replicated
The draws below stay inside these ranges and needn't reach their ends.
All inputs are finite; a program needn't handle non-finite values.
Results may differ from the reference program's by a relative error of at most 0.006.
Values may be sent and summed in bfloat16 or wider, within the bound.
A program may use at most 64 MiB of HBM per device.

```python
import jax
import jax.numpy as jnp
from jax import lax

C = 64
H = 16
W = 24
PATIENTS = 8
NZ = 192


def rough_volume(key, depth_slope):
    subkeys = jax.random.split(key, 3)
    raw_values = jnp.clip(jax.random.normal(subkeys[0], (PATIENTS, C, NZ, H * W), jnp.float32), -4.0, 4.0)
    depth_frac = jnp.arange(NZ, dtype=jnp.float32) / max(NZ - 1, 1)
    cell_exp = jax.random.uniform(subkeys[1], (PATIENTS, 1, NZ, H * W), jnp.float32, 0.0, 0.5)
    chan_exp = jax.random.uniform(subkeys[2], (PATIENTS, C, 1, 1), jnp.float32, 0.0, 0.5)
    magnitude = 10.0 ** (depth_slope * depth_frac[None, None, :, None] + cell_exp + chan_exp - 0.5 * (depth_slope + 1.0))
    return raw_values * magnitude


def draw_features(key, part):
    return rough_volume(jax.random.fold_in(key, 11), 0.48).astype(jnp.bfloat16)


def draw_cotangent(key, part):
    return rough_volume(jax.random.fold_in(key, 23), 0.48).astype(jnp.bfloat16)


def centred(own_key, extent, scale, most, kind=jnp.bfloat16):
    array = jax.random.normal(own_key, extent, jnp.float32) * scale
    return jnp.minimum(jnp.maximum(array, -most), most).astype(kind)


def setup_inputs(seed: int = 0) -> dict:
    streams_of = jax.random.split(jax.random.key(seed), 6)
    features = draw_features(jax.random.fold_in(streams_of[5], 71), 0)
    cotangent = draw_cotangent(jax.random.fold_in(streams_of[5], 71), 0)
    weights = centred(streams_of[2], (2, C, 27 * C), (27 * C) ** -0.5, 0.15625, jnp.float32)
    prev_state = centred(streams_of[3], (2, C, 27 * C), 1.0, 6.0, jnp.float32)
    tree_noise = centred(streams_of[4], (2, C, 27 * C), 1.0, 6.0, jnp.float32)
    return dict(features=features, cotangent=cotangent, weights=weights, prev_state=prev_state, tree_noise=tree_noise)


eps_norm = 1e-05
clip_bound = 400.0
step_rate = 0.1

def convolve(volume, kernel):
    channels = kernel.shape[0]
    filters = kernel.reshape(channels, 3, 3, 3, channels).transpose(0, 4, 1, 2, 3)
    result = lax.conv_general_dilated(volume[None], filters, (1, 1, 1), ((1, 1), (1, 1), (1, 1)), dimension_numbers=('NCDHW', 'OIDHW', 'NCDHW'), precision=lax.Precision.HIGHEST)
    return result[0]

def normalize(summed):
    centre = lax.optimization_barrier(jnp.mean(summed, axis=(1, 2, 3), keepdims=True))
    squares = lax.optimization_barrier(jnp.mean(summed * summed, axis=(1, 2, 3), keepdims=True))
    spread = lax.rsqrt(squares - centre * centre + eps_norm)
    return ((summed - centre) * spread, spread)

def norm_back(gradient, normed, spread):
    first = lax.optimization_barrier(jnp.mean(gradient, axis=(1, 2, 3), keepdims=True))
    second = lax.optimization_barrier(jnp.mean(gradient * normed, axis=(1, 2, 3), keepdims=True))
    return spread * (gradient - first - normed * second)

def silu_slope(values):
    sigmoid_val = jax.nn.sigmoid(values)
    return sigmoid_val * (1.0 + values * (1.0 - sigmoid_val))

def to_half(values):
    rounded = lax.optimization_barrier(values.astype(jnp.bfloat16))
    return rounded.astype(jnp.float32)

def patient_grad(volume, upstream, kernel_one, kernel_two):
    channels, planes, plane_size = volume.shape
    shaped = (channels, planes, H, W)
    inputs = volume.astype(jnp.float32).reshape(shaped)
    normed_one, spread_one = normalize(convolve(inputs, kernel_one))
    hidden = to_half(jax.nn.silu(normed_one))
    normed_two, spread_two = normalize(convolve(hidden, kernel_two))
    gradient_two = upstream.astype(jnp.float32).reshape(shaped) * silu_slope(normed_two)
    cotan_two = to_half(norm_back(gradient_two, normed_two, spread_two))
    unused, pull_two = jax.vjp(convolve, hidden, kernel_two)
    back_hidden, kgrad_two = pull_two(cotan_two)
    gradient_one = back_hidden * silu_slope(normed_one)
    cotan_one = to_half(norm_back(gradient_one, normed_one, spread_one))

    def first_layer(kernel):
        return convolve(inputs, kernel)
    unused_one, pull_one = jax.vjp(first_layer, kernel_one)
    kgrad_one = pull_one(cotan_one)[0]
    return jnp.stack([kgrad_one, kgrad_two])

def reference(features, cotangent, weights, prev_state, tree_noise):
    kernels = to_half(weights)

    def accumulate(running, patient):
        gradient = patient_grad(patient[0], patient[1], kernels[0], kernels[1])
        length = jnp.sqrt(jnp.sum(gradient * gradient))
        factor = clip_bound / jnp.maximum(length, clip_bound)
        return (running + factor * gradient, None)
    combined, unused = lax.scan(accumulate, jnp.zeros(weights.shape, jnp.float32), (features, cotangent))
    state_next = prev_state + combined
    weights_next = weights - step_rate * (combined + tree_noise)
    return (state_next, weights_next)
```

```python
import jax
import jax.numpy as jnp
from jax import lax
from jax.experimental import pallas as pl
from jax.experimental.pallas import tpu as pltpu
from jax.sharding import PartitionSpec as P

MESH = pl.DeviceIdType.MESH
C = 64
W = 24
CELLS = 384
PLANES = 6
WIDE = PLANES + 2
TAPS = 9
ROWS = TAPS * C
PADDED = 640
SLABS = 32
PATS = 8
OWNERS = 30
LANE_TILES = 5
BLOCK = (32, 128)
EPS = 1e-05
CLIP = 400.0
RATE = 0.1
COUNT = SLABS * PLANES * CELLS
F32 = jnp.float32
BF16 = jnp.bfloat16


def sigmoid(v):
    return 1.0 / (1.0 + jnp.exp(-v))


def plane(j):
    if isinstance(j, int):
        return pl.ds(j * CELLS, CELLS)
    return pl.ds(pl.multiple_of(j * CELLS, 128), CELLS)


def kernel(
    feat_ref, cot_ref, w_ref, out_ref,
    spread32, feat, cot, masks, kst, kback, im_feat, im_hid, im_cot, parts, normed_one, normed_two, grad,
    lhs, acc, feat_halo, cot_halo, first_halo, second_halo, edge, rows_out, slots, kg, reduced, scaled, pat_slots, gathered,
    halo_send, halo_recv, row_send, row_recv, red_send, red_recv, pat_send, pat_recv, ag_send, ag_recv, core_send, core_recv,
):
    p = lax.axis_index("pat")
    s = lax.axis_index("slab")
    core = lax.rem(p, 2)

    def slab_peer(k):
        return (p, lax.rem(s + k, SLABS))

    def pat_peer(k):
        return (lax.rem(p + k, PATS), s)

    barrier = pltpu.get_barrier_semaphore()

    @pl.loop(1, SLABS)
    def _(k):
        pl.semaphore_signal(barrier, inc=1, device_id=slab_peer(k), device_id_type=MESH)

    @pl.loop(1, PATS)
    def _(k):
        pl.semaphore_signal(barrier, inc=1, device_id=pat_peer(k), device_id_type=MESH)

    def halo_copies(stage, low, high, landing):
        return (
            pltpu.make_async_remote_copy(
                low, landing.at[1], halo_send.at[stage, 0], halo_recv.at[stage, 1],
                device_id=slab_peer(SLABS - 1), device_id_type=MESH,
            ),
            pltpu.make_async_remote_copy(
                high, landing.at[0], halo_send.at[stage, 1], halo_recv.at[stage, 0],
                device_id=slab_peer(1), device_id_type=MESH,
            ),
        )

    def kept(j):
        cut = ((j == 0) & (s == 0)) | ((j == WIDE - 1) & (s == SLABS - 1))
        return jnp.where(cut, 0.0, 1.0).astype(F32)

    def eye():
        i = lax.broadcasted_iota(jnp.int32, (128, 128), 0)
        j = lax.broadcasted_iota(jnp.int32, (128, 128), 1)
        return i == j

    def share_row(r, row):
        rows_out[r] = row

        @pl.loop(1, SLABS)
        def _(k):
            pltpu.make_async_remote_copy(
                rows_out.at[r], slots.at[r, s], row_send.at[r], row_recv.at[r],
                device_id=slab_peer(k), device_id_type=MESH,
            ).start()

        slots[r, s] = row

    def row_total(r):
        most = slots.at[r, pl.ds(0, SLABS - 1)]
        pltpu.make_async_copy(most, most, row_recv.at[r]).wait()
        return jnp.sum(slots[r], axis=0)

    def share_pair(r, one, two):
        column = jnp.concatenate([one, two], axis=0)
        share_row(r, jnp.sum(jnp.where(eye(), column, 0.0), axis=0, keepdims=True))

    def pair_total(r):
        row = row_total(r) * (1.0 / COUNT)
        column = jnp.sum(jnp.where(eye(), row, 0.0), axis=1, keepdims=True)
        return column[:C], column[C:]

    def taps(values, im, j):
        for t in range(TAPS):
            shift = (t // 3 - 1) * W + (t % 3 - 1)
            if shift == 0:
                piece = values
            else:
                piece = pltpu.roll(values, (-shift) % CELLS, 1)
                piece = (piece.reshape(C // 16, 16, CELLS) * masks[t]).reshape(C, CELLS)
            im[t * C : (t + 1) * C, plane(j)] = piece

    def multiply(matrix, im, start, width):
        columns = pl.ds(start if isinstance(start, int) else pl.multiple_of(start, 128), width)
        parts[:, columns] = jnp.dot(matrix, im[0:ROWS, columns], preferred_element_type=F32)

    def combined(j):
        return (
            parts[0:C, plane(j)]
            + parts[C : 2 * C, plane(j + 1)]
            + parts[2 * C : 3 * C, plane(j + 2)]
        )

    def lane_sum(v):
        return v[:, 0:128] + v[:, 128:256] + v[:, 256:384]

    spread32[...] = feat_ref[0].astype(F32)
    for z in range(PLANES):
        feat[:, plane(z + 1)] = spread32[:, z, :].astype(BF16)
    spread32[...] = cot_ref[0].astype(F32)
    for z in range(PLANES):
        cot[:, plane(z + 1)] = spread32[:, z, :].astype(BF16)
    for side, j in ((0, 1), (1, PLANES)):
        edge[side] = feat[:, plane(j)]
        edge[2 + side] = cot[:, plane(j)]

    cell = lax.broadcasted_iota(jnp.int32, (16, CELLS), 1)
    row, col = lax.div(cell, W), lax.rem(cell, W)
    for t in range(TAPS):
        b, e = t // 3 - 1, t % 3 - 1
        inside = (row + b >= 0) & (row + b < CELLS // W) & (col + e >= 0) & (col + e < W)
        masks[t] = jnp.where(inside, 1.0, 0.0).astype(BF16)
    for a in range(3):
        for k in range(2):
            kst[k, a * C : (a + 1) * C, :] = w_ref[k, :, a * ROWS : (a + 1) * ROWS].astype(BF16)
    for im in (im_feat, im_hid):
        im[ROWS:PADDED, :] = jnp.zeros((PADDED - ROWS, WIDE * CELLS), BF16)

    @pl.loop(1, WIDE - 1)
    def _(j):
        taps(feat[:, plane(j)], im_feat, j)

    @pl.loop(0, 3)
    def _(c):
        multiply(kst[0], im_feat, CELLS + c * 2 * CELLS, 2 * CELLS)

    turned = jnp.transpose(w_ref[1].astype(BF16).astype(F32))
    for a in range(3):
        for t in range(TAPS):
            block = turned[(a * TAPS + t) * C : (a * TAPS + t + 1) * C, :]
            u = TAPS - 1 - t
            kback[(2 - a) * C : (3 - a) * C, u * C : (u + 1) * C] = block.astype(BF16)
    for a in range(3):
        for j in range(WIDE):
            if not a <= j < a + PLANES:
                lhs[a * C : (a + 1) * C, plane(j)] = jnp.zeros((C, CELLS), BF16)

    pl.semaphore_wait(barrier, SLABS - 1 + PATS - 1)

    halos = [halo_copies(0, edge.at[0], edge.at[1], feat_halo), halo_copies(1, edge.at[2], edge.at[3], cot_halo)]
    for pair in halos:
        for copy in pair:
            copy.start()
    for copy in halos[0]:
        copy.wait_recv()
    for side, j in ((0, 0), (1, WIDE - 1)):
        taps(feat_halo[side] * kept(j).astype(BF16), im_feat, j)
        multiply(kst[0], im_feat, j * CELLS, CELLS)

    def convolved(target):
        def body(j, carry):
            value = combined(j)
            target[:, plane(j + 1)] = value
            return carry[0] + lane_sum(value), carry[1] + lane_sum(value * value)

        zero = jnp.zeros((C, 128), F32)
        one, two = lax.fori_loop(0, PLANES, body, (zero, zero))
        return jnp.sum(one, axis=1, keepdims=True), jnp.sum(two, axis=1, keepdims=True)

    def exchange(stage, field, landing):
        pair = halo_copies(stage, field.at[:, plane(1)], field.at[:, plane(PLANES)], landing)
        for copy in pair:
            copy.start()
        return pair

    share_pair(0, *convolved(normed_one))
    pair = exchange(2, normed_one, first_halo)
    centre_one, squares = pair_total(0)
    spread_one = lax.rsqrt(squares - centre_one * centre_one + EPS)
    for copy in pair:
        copy.wait()
    normed_one[:, plane(0)] = first_halo[0]
    normed_one[:, plane(WIDE - 1)] = first_halo[1]

    @pl.loop(0, WIDE)
    def _(j):
        value = (normed_one[:, plane(j)] - centre_one) * spread_one
        normed_one[:, plane(j)] = value
        taps((value * sigmoid(value) * kept(j)).astype(BF16), im_hid, j)

    @pl.loop(0, 4)
    def _(c):
        multiply(kst[1], im_hid, c * 2 * CELLS, 2 * CELLS)

    share_pair(1, *convolved(normed_two))
    pair = exchange(3, normed_two, second_halo)
    centre_two, squares = pair_total(1)
    spread_two = lax.rsqrt(squares - centre_two * centre_two + EPS)
    for copy in halos[1]:
        copy.wait()
    for copy in pair:
        copy.wait()
    normed_two[:, plane(0)] = second_halo[0]
    normed_two[:, plane(WIDE - 1)] = second_halo[1]
    cot[:, plane(0)] = cot_halo[0]
    cot[:, plane(WIDE - 1)] = cot_halo[1]

    def slope(v):
        h = sigmoid(v)
        return h * (1.0 + v * (1.0 - h))

    def second_gradient(j, carry):
        value = (normed_two[:, plane(j)] - centre_two) * spread_two
        normed_two[:, plane(j)] = value
        g = cot[:, plane(j)].astype(F32) * slope(value)
        grad[:, plane(j)] = g
        return carry[0] + lane_sum(g), carry[1] + lane_sum(g * value)

    zero = jnp.zeros((C, 128), F32)
    one, two = lax.fori_loop(1, WIDE - 1, second_gradient, (zero, zero))
    share_pair(2, jnp.sum(one, axis=1, keepdims=True), jnp.sum(two, axis=1, keepdims=True))
    second_gradient(0, (zero, zero))
    second_gradient(WIDE - 1, (zero, zero))
    mean_two, cross_two = pair_total(2)

    @pl.loop(0, WIDE)
    def _(j):
        value = spread_two * (grad[:, plane(j)] - mean_two - normed_two[:, plane(j)] * cross_two)
        value = (value * kept(j)).astype(BF16)
        cot[:, plane(j)] = value
        taps(value, im_cot, j)

    @pl.loop(0, 4)
    def _(c):
        multiply(kback[...], im_cot, c * 2 * CELLS, 2 * CELLS)

    def first_gradient(j, carry):
        value = normed_one[:, plane(j + 1)]
        g = combined(j) * slope(value)
        grad[:, plane(j + 1)] = g
        return carry[0] + lane_sum(g), carry[1] + lane_sum(g * value)

    one, two = lax.fori_loop(0, PLANES, first_gradient, (zero, zero))
    share_pair(3, jnp.sum(one, axis=1, keepdims=True), jnp.sum(two, axis=1, keepdims=True))

    def kernel_gradient(k, im):
        @pl.loop(0, 4)
        def _(c):
            columns = pl.ds(pl.multiple_of(c * 2 * CELLS, 128), 2 * CELLS)
            term = lax.dot_general(
                lhs[:, columns], im[:, columns], (((1,), (1,)), ((), ())), preferred_element_type=F32
            )

            @pl.when(c == 0)
            def _():
                acc[...] = term

            @pl.when(c > 0)
            def _():
                acc[...] += term

        for rg in range(6):
            for lt in range(LANE_TILES):
                kg[k, rg * LANE_TILES + lt] = acc[rg * 32 : (rg + 1) * 32, lt * 128 : (lt + 1) * 128]

        @pl.loop(1, SLABS)
        def _(q):
            owner = lax.rem(s + q, SLABS)

            @pl.when(owner < OWNERS)
            def _():
                pltpu.make_async_remote_copy(
                    kg.at[k, owner], reduced.at[k, s], red_send.at[k], red_recv.at[k],
                    device_id=(p, owner), device_id_type=MESH,
                ).start()

        @pl.when(s < OWNERS)
        def _():
            reduced[k, s] = kg[k, s]

    def place(j, value):
        for a in range(3):
            lhs[a * C : (a + 1) * C, plane(j + a)] = value

    @pl.loop(0, PLANES)
    def _(j):
        place(j, cot[:, plane(j + 1)])

    kernel_gradient(1, im_hid)
    mean_one, cross_one = pair_total(3)

    @pl.loop(0, PLANES)
    def _(j):
        value = spread_one * (grad[:, plane(j + 1)] - mean_one - normed_one[:, plane(j + 1)] * cross_one)
        place(j, value.astype(BF16))

    kernel_gradient(0, im_feat)

    def wait_blocks(ref, sem):
        pltpu.make_async_copy(ref, ref, sem).wait()

    @pl.when(s < OWNERS)
    def _():
        for k in (1, 0):
            wait_blocks(reduced.at[k, pl.ds(0, SLABS - 1)], red_recv.at[k])
            scaled[k] = lax.fori_loop(0, SLABS, lambda q, total: total + reduced[k, q], jnp.zeros(BLOCK, F32))

    @pl.when(s >= OWNERS)
    def _():
        for k in (0, 1):
            scaled[k] = jnp.zeros(BLOCK, F32)

    squared = jnp.sum(scaled[0] * scaled[0] + scaled[1] * scaled[1], axis=0, keepdims=True)
    share_row(4, squared)
    length = jnp.sqrt(jnp.sum(row_total(4), axis=1, keepdims=True))
    factor = CLIP / jnp.maximum(length, CLIP)
    for k in (0, 1):
        scaled[k] = scaled[k] * factor

    @pl.when(s < OWNERS)
    def _():
        @pl.loop(1, PATS)
        def _(q):
            peer = lax.rem(p + q, PATS)
            pltpu.make_async_remote_copy(
                scaled.at[lax.rem(peer, 2)], pat_slots.at[p], pat_send, pat_recv,
                device_id=(peer, s), device_id_type=MESH,
            ).start()

        pat_slots[p] = scaled[core]
        wait_blocks(pat_slots.at[pl.ds(0, PATS - 1)], pat_recv)
        total = pat_slots[0]
        for q in range(1, PATS):
            total = total + pat_slots[q]
        gathered[core, s] = total

        @pl.loop(1, SLABS)
        def _(q):
            pltpu.make_async_remote_copy(
                gathered.at[core, s], gathered.at[core, s], ag_send, ag_recv,
                device_id=slab_peer(q), device_id_type=MESH,
            ).start()

        wait_blocks(gathered.at[0, pl.ds(0, OWNERS - 1)], ag_recv)

    @pl.when(s >= OWNERS)
    def _():
        wait_blocks(gathered.at[0, pl.ds(0, OWNERS)], ag_recv)

    last = pltpu.make_async_remote_copy(
        gathered.at[core], gathered.at[core], core_send, core_recv,
        device_id=(p + 1 - 2 * core, s), device_id_type=MESH,
    )
    last.start()
    last.wait()

    for k in range(2):
        for a in range(3):
            for h in range(2):
                for lt in range(LANE_TILES):
                    width = 128 if lt < LANE_TILES - 1 else C
                    start = a * ROWS + lt * 128
                    block = gathered[k, (2 * a + h) * LANE_TILES + lt]
                    out_ref[k, h * 32 : (h + 1) * 32, start : start + width] = block[:, :width]

    for copy in halos[0]:
        copy.wait_send()
    for r in range(5):
        wait_blocks(slots.at[r, pl.ds(0, SLABS - 1)], row_send.at[r])

    @pl.when(s < OWNERS)
    def _():
        for k in range(2):
            wait_blocks(kg.at[k, pl.ds(0, OWNERS - 1)], red_send.at[k])
        wait_blocks(pat_slots.at[pl.ds(0, PATS - 1)], pat_send)
        wait_blocks(reduced.at[0, pl.ds(0, SLABS - 1)], ag_send)

    @pl.when(s >= OWNERS)
    def _():
        for k in range(2):
            wait_blocks(kg.at[k, pl.ds(0, OWNERS)], red_send.at[k])


def clipped_gradients(features, cotangent, weights):
    wide = WIDE * CELLS
    vmem, dma = pltpu.VMEM, pltpu.SemaphoreType.DMA
    return pl.pallas_call(
        kernel,
        out_shape=jax.ShapeDtypeStruct((2, C, 3 * ROWS), F32),
        in_specs=[pl.BlockSpec(memory_space=vmem)] * 3,
        out_specs=pl.BlockSpec(memory_space=vmem),
        scratch_shapes=[
            vmem((C, PLANES, CELLS), F32),
            vmem((C, wide), BF16),
            vmem((C, wide), BF16),
            vmem((TAPS, 16, CELLS), BF16),
            vmem((2, 3 * C, ROWS), BF16),
            vmem((3 * C, ROWS), BF16),
            vmem((PADDED, wide), BF16),
            vmem((PADDED, wide), BF16),
            vmem((ROWS, wide), BF16),
            vmem((3 * C, wide), F32),
            vmem((C, wide), F32),
            vmem((C, wide), F32),
            vmem((C, wide), F32),
            vmem((3 * C, wide), BF16),
            vmem((3 * C, PADDED), F32),
            vmem((2, C, CELLS), BF16),
            vmem((2, C, CELLS), BF16),
            vmem((2, C, CELLS), F32),
            vmem((2, C, CELLS), F32),
            vmem((4, C, CELLS), BF16),
            vmem((5, 1, 128), F32),
            vmem((5, SLABS, 1, 128), F32),
            vmem((2, OWNERS) + BLOCK, F32),
            vmem((2, SLABS) + BLOCK, F32),
            vmem((2,) + BLOCK, F32),
            vmem((PATS,) + BLOCK, F32),
            vmem((2, OWNERS) + BLOCK, F32),
            dma((4, 2)), dma((4, 2)), dma((5,)), dma((5,)), dma((2,)), dma((2,)), dma, dma, dma, dma, dma, dma,
        ],
        compiler_params=pltpu.CompilerParams(
            collective_id=0, has_side_effects=True, vmem_limit_bytes=48 * 1024 * 1024
        ),
    )(features, cotangent, weights)


def per_device(features, cotangent, weights, prev_state, tree_noise):
    total = clipped_gradients(features, cotangent, weights)
    return prev_state + total, weights - RATE * (total + tree_noise)


def solution(mesh):
    return jax.shard_map(
        per_device,
        mesh=mesh,
        in_specs=(P("pat", None, "slab", None), P("pat", None, "slab", None), P(), P(), P()),
        out_specs=(P(), P()),
        check_vma=False,
    )
```

```python
import jax
import jax.numpy as jnp
from jax import lax
from jax.experimental import pallas as pl
from jax.experimental.pallas import tpu as pltpu
from jax.sharding import PartitionSpec as P

MESH = pl.DeviceIdType.MESH
C = 64
W = 24
CELLS = 384
PLANES = 6
WIDE = PLANES + 2
TAPS = 9
ROWS = TAPS * C
PADDED = 640
SLABS = 32
PATS = 8
OWNERS = 27
LANE_TILES = 9
BLOCK = (32, 128)
EPS = 1e-05
CLIP = 400.0
RATE = 0.1
COUNT = SLABS * PLANES * CELLS
F32 = jnp.float32
BF16 = jnp.bfloat16


def sigmoid(v):
    return 1.0 / (1.0 + jnp.exp(-v))


def plane(j, count=1):
    return slice(j * CELLS, (j + count) * CELLS)


def kernel(
    feat_hbm, cot_hbm, w_hbm, out_ref,
    feat_ref, cot_ref, w_ref,
    cot, masks, kst, kback, im_feat, im_hid, im_cot, parts, normed_one, normed_two, grad,
    lhs, acc, feat_halo, cot_halo, first_halo, second_halo, rows_out, slots, kg, reduced, scaled, pat_slots, gathered, lengths,
    halo_send, halo_recv, row_send, row_recv, red_send, red_recv, pat_send, pat_recv, len_send, len_recv, ag_send, ag_recv, core_send, core_recv, load_sem,
):
    p = lax.axis_index("pat")
    s = lax.axis_index("slab")
    core = lax.rem(p, 2)

    def slab_peer(k):
        return (p, lax.rem(s + k, SLABS))

    def pat_peer(k):
        return (lax.rem(p + k, PATS), s)

    pending = []
    barrier = pltpu.get_barrier_semaphore()

    @pl.loop(1, SLABS)
    def _(k):
        pl.semaphore_signal(barrier, inc=1, device_id=slab_peer(k), device_id_type=MESH)

    @pl.loop(1, PATS)
    def _(k):
        pl.semaphore_signal(barrier, inc=1, device_id=pat_peer(k), device_id_type=MESH)

    loads = [
        pltpu.make_async_copy(source, target, load_sem.at[i])
        for i, (source, target) in enumerate(((feat_hbm, feat_ref), (w_hbm, w_ref), (cot_hbm, cot_ref)))
    ]
    for load in loads:
        load.start()

    def halo_copies(stage, low, high, landing):
        return (
            pltpu.make_async_remote_copy(
                low, landing.at[1], halo_send.at[stage, 0], halo_recv.at[stage, 1],
                device_id=slab_peer(SLABS - 1), device_id_type=MESH,
            ),
            pltpu.make_async_remote_copy(
                high, landing.at[0], halo_send.at[stage, 1], halo_recv.at[stage, 0],
                device_id=slab_peer(1), device_id_type=MESH,
            ),
        )

    def wait_blocks(ref, sem):
        pltpu.make_async_copy(ref, ref, sem).wait()

    def wait_owned(ref, sem):
        @pl.when(s < OWNERS)
        def _():
            wait_blocks(ref.at[pl.ds(0, OWNERS - 1)], sem)

        @pl.when(s >= OWNERS)
        def _():
            wait_blocks(ref.at[pl.ds(0, OWNERS)], sem)

    def wait_red(k):
        @pl.when(s < OWNERS)
        def _():
            wait_blocks(reduced.at[k, pl.ds(0, SLABS - 1)], red_recv.at[k])

    def kept(j):
        if 0 < j < WIDE - 1:
            return 1.0
        return jnp.where(s == (0 if j == 0 else SLABS - 1), 0.0, 1.0).astype(F32)

    def eye():
        i = lax.broadcasted_iota(jnp.int32, (128, 128), 0)
        j = lax.broadcasted_iota(jnp.int32, (128, 128), 1)
        return i == j

    def share_row(r, row):
        rows_out[r] = row

        @pl.loop(1, SLABS)
        def _(k):
            pltpu.make_async_remote_copy(
                rows_out.at[r], slots.at[r, s], row_send.at[r], row_recv.at[r],
                device_id=slab_peer(k), device_id_type=MESH,
            ).start()

        slots[r, s] = row
        pending.append(lambda: wait_blocks(slots.at[r, pl.ds(0, SLABS - 1)], row_send.at[r]))

    def row_total(r):
        most = slots.at[r, pl.ds(0, SLABS - 1)]
        pltpu.make_async_copy(most, most, row_recv.at[r]).wait()
        return jnp.sum(slots[r], axis=0)

    def share_pair(r, one, two):
        column = jnp.concatenate([one, two], axis=0)
        share_row(r, jnp.sum(jnp.where(eye(), column, 0.0), axis=0, keepdims=True))

    def pair_total(r):
        row = row_total(r) * (1.0 / COUNT)
        column = jnp.sum(jnp.where(eye(), row, 0.0), axis=1, keepdims=True)
        return column[:C], column[C:]

    def taps(values, im, j):
        for t in range(TAPS):
            shift = (t // 3 - 1) * W + (t % 3 - 1)
            if shift == 0:
                piece = values
            else:
                piece = pltpu.roll(values, (-shift) % CELLS, 1)
                piece = (piece.reshape(C // 16, 16, CELLS) * masks[t]).reshape(C, CELLS)
            im[t * C : (t + 1) * C, plane(j)] = piece

    def multiply(matrix, im, first, count):
        parts[:, plane(first, count)] = jnp.dot(matrix, im[0:ROWS, plane(first, count)], preferred_element_type=F32)

    def combined(j):
        return (
            parts[0:C, plane(j)]
            + parts[C : 2 * C, plane(j + 1)]
            + parts[2 * C : 3 * C, plane(j + 2)]
        )

    def lane_sum(v):
        return v[:, 0:128] + v[:, 128:256] + v[:, 256:384]

    cell = lax.broadcasted_iota(jnp.int32, (16, CELLS), 1)
    row, col = lax.div(cell, W), lax.rem(cell, W)
    for t in range(TAPS):
        b, e = t // 3 - 1, t % 3 - 1
        inside = (row + b >= 0) & (row + b < CELLS // W) & (col + e >= 0) & (col + e < W)
        masks[t] = jnp.where(inside, 1.0, 0.0).astype(BF16)
    loads[1].wait()
    for a in range(3):
        kst[0, a * C : (a + 1) * C, :] = w_ref[0, :, a * ROWS : (a + 1) * ROWS].astype(BF16)
    loads[0].wait()
    for j in range(1, WIDE - 1):
        taps(feat_ref[j - 1], im_feat, j)
    loads[2].wait()
    pl.semaphore_wait(barrier, SLABS - 1 + PATS - 1)

    halos = [halo_copies(0, feat_ref.at[0], feat_ref.at[PLANES - 1], feat_halo), halo_copies(1, cot_ref.at[0], cot_ref.at[PLANES - 1], cot_halo)]
    for pair in halos:
        for copy in pair:
            copy.start()
    multiply(kst[0], im_feat, 1, PLANES)
    for copy in halos[0]:
        copy.wait_recv()
        pending.append(copy.wait_send)
    for side, j, a in ((0, 0, 0), (1, WIDE - 1, 2)):
        taps(feat_halo[side] * kept(j).astype(BF16), im_feat, j)
        parts[a * C : (a + 1) * C, plane(j)] = jnp.dot(
            kst[0, a * C : (a + 1) * C, :], im_feat[0:ROWS, plane(j)], preferred_element_type=F32
        )

    def convolved(target, stage, landing):
        one = two = jnp.zeros((C, 128), F32)
        for z in (0, PLANES - 1, 1, 2, 3, 4):
            value = combined(z)
            target[:, plane(z + 1)] = value
            one, two = one + lane_sum(value), two + lane_sum(value * value)
            if z == PLANES - 1:
                pair = halo_copies(stage, target.at[:, plane(1)], target.at[:, plane(PLANES)], landing)
                for copy in pair:
                    copy.start()
        return pair, jnp.sum(one, axis=1, keepdims=True), jnp.sum(two, axis=1, keepdims=True)

    pair, *sums = convolved(normed_one, 2, first_halo)
    share_pair(0, *sums)

    for a in range(3):
        kst[1, a * C : (a + 1) * C, :] = w_ref[1, :, a * ROWS : (a + 1) * ROWS].astype(BF16)
    turned = jnp.transpose(w_ref[1].astype(BF16).astype(F32))
    for a in range(3):
        for t in range(TAPS):
            block = turned[(a * TAPS + t) * C : (a * TAPS + t + 1) * C, :]
            u = TAPS - 1 - t
            kback[(2 - a) * C : (3 - a) * C, u * C : (u + 1) * C] = block.astype(BF16)
        for j in range(WIDE):
            if not a <= j < a + PLANES:
                lhs[a * C : (a + 1) * C, plane(j)] = jnp.zeros((C, CELLS), BF16)
    for im in (im_feat, im_hid):
        im[ROWS:PADDED, :] = jnp.zeros((PADDED - ROWS, WIDE * CELLS), BF16)

    centre_one, squares = pair_total(0)
    spread_one = lax.rsqrt(squares - centre_one * centre_one + EPS)
    for copy in pair:
        copy.wait()
    normed_one[:, plane(0)] = first_halo[0]
    normed_one[:, plane(WIDE - 1)] = first_halo[1]

    for j in range(WIDE):
        value = (normed_one[:, plane(j)] - centre_one) * spread_one
        normed_one[:, plane(j)] = value
        taps((value * sigmoid(value) * kept(j)).astype(BF16), im_hid, j)
        if j % 2:
            multiply(kst[1], im_hid, j - 1, 2)

    pair, *sums = convolved(normed_two, 3, second_halo)
    share_pair(1, *sums)
    centre_two, squares = pair_total(1)
    spread_two = lax.rsqrt(squares - centre_two * centre_two + EPS)
    for copy in halos[1]:
        copy.wait()
    for copy in pair:
        copy.wait()
    normed_two[:, plane(0)] = second_halo[0]
    normed_two[:, plane(WIDE - 1)] = second_halo[1]

    def slope(v):
        h = sigmoid(v)
        return h * (1.0 + v * (1.0 - h))

    def second_gradient(j, carry, upstream=None):
        value = (normed_two[:, plane(j)] - centre_two) * spread_two
        normed_two[:, plane(j)] = value
        upstream = cot_ref[j - 1] if upstream is None else upstream
        g = upstream.astype(F32) * slope(value)
        grad[:, plane(j)] = g
        return carry[0] + lane_sum(g), carry[1] + lane_sum(g * value)

    zero = jnp.zeros((C, 128), F32)
    carry = (zero, zero)
    for j in range(1, WIDE - 1):
        carry = second_gradient(j, carry)
    one, two = carry
    share_pair(2, jnp.sum(one, axis=1, keepdims=True), jnp.sum(two, axis=1, keepdims=True))
    second_gradient(0, (zero, zero), cot_halo[0])
    second_gradient(WIDE - 1, (zero, zero), cot_halo[1])
    mean_two, cross_two = pair_total(2)

    for j in range(WIDE):
        value = spread_two * (grad[:, plane(j)] - mean_two - normed_two[:, plane(j)] * cross_two)
        value = (value * kept(j)).astype(BF16)
        cot[:, plane(j)] = value
        taps(value, im_cot, j)
        if j % 2:
            multiply(kback[...], im_cot, j - 1, 2)

    def first_gradient(j, carry):
        value = normed_one[:, plane(j + 1)]
        g = combined(j) * slope(value)
        grad[:, plane(j + 1)] = g
        return carry[0] + lane_sum(g), carry[1] + lane_sum(g * value)

    carry = (zero, zero)
    for z in range(PLANES):
        carry = first_gradient(z, carry)
    one, two = carry
    share_pair(3, jnp.sum(one, axis=1, keepdims=True), jnp.sum(two, axis=1, keepdims=True))

    def kernel_gradient(k, im):
        def send(first, count):
            for a in range(3):
                for t in range(first, first + count):
                    owner = a * LANE_TILES + t

                    @pl.when(s != owner)
                    def _():
                        pltpu.make_async_remote_copy(
                            kg.at[k, owner], reduced.at[k, s], red_send.at[k], red_recv.at[k],
                            device_id=(p, owner), device_id_type=MESH,
                        ).start()

        for first in (0, 256, 512):
            width = 256 if first < 512 else 128
            term = lax.dot_general(
                lhs[...], im[first : first + width, :], (((1,), (1,)), ((), ())), preferred_element_type=F32
            )
            for a in range(3):
                low, high = term[a * C : a * C + 32], term[a * C + 32 : (a + 1) * C]
                if first < 512:
                    for t in range(2):
                        lanes = slice(t * 128, (t + 1) * 128)
                        kg[k, a * LANE_TILES + first // 128 + t] = low[:, lanes].astype(BF16)
                        kg[k, a * LANE_TILES + 4 + first // 128 + t] = high[:, lanes].astype(BF16)
                else:
                    kg[k, a * LANE_TILES + 8] = (low + pltpu.roll(high, C, 1)).astype(BF16)
            if first < 512:
                send(first // 128, 2)
                send(4 + first // 128, 2)
            else:
                send(8, 1)

        @pl.when(s < OWNERS)
        def _():
            reduced[k, s] = kg[k, s]

        pending.append(lambda: wait_owned(kg.at[k], red_send.at[k]))

    def place(j, value):
        for a in range(3):
            lhs[a * C : (a + 1) * C, plane(j + a)] = value

    for j in range(PLANES):
        place(j, cot[:, plane(j + 1)])

    kernel_gradient(1, im_hid)
    mean_one, cross_one = pair_total(3)

    for j in range(PLANES):
        value = spread_one * (grad[:, plane(j + 1)] - mean_one - normed_one[:, plane(j + 1)] * cross_one)
        place(j, value.astype(BF16))

    kernel_gradient(0, im_feat)

    @pl.when(s < OWNERS)
    def _():
        for k in (1, 0):
            wait_red(k)
            scaled[k] = lax.fori_loop(0, SLABS, lambda q, total: total + reduced[k, q].astype(F32), jnp.zeros(BLOCK, F32))

    @pl.when(s >= OWNERS)
    def _():
        for k in (0, 1):
            scaled[k] = jnp.zeros(BLOCK, F32)

    squared = jnp.sum(scaled[0] * scaled[0] + scaled[1] * scaled[1], axis=0, keepdims=True)
    share_row(4, squared)

    @pl.when(s < OWNERS)
    def _():
        @pl.loop(1, PATS)
        def _(q):
            peer = lax.rem(p + q, PATS)
            pltpu.make_async_remote_copy(
                scaled.at[lax.rem(peer, 2)], pat_slots.at[p], pat_send, pat_recv,
                device_id=(peer, s), device_id_type=MESH,
            ).start()

        pat_slots[p] = scaled[core]

    lengths[p] = row_total(4)

    @pl.when(s < OWNERS)
    def _():
        @pl.loop(1, PATS)
        def _(q):
            pltpu.make_async_remote_copy(
                lengths.at[p], lengths.at[p], len_send, len_recv, device_id=pat_peer(q), device_id_type=MESH
            ).start()

        wait_blocks(pat_slots.at[pl.ds(0, PATS - 1)], pat_recv)
        wait_blocks(lengths.at[pl.ds(0, PATS - 1)], len_recv)
        wait_blocks(lengths.at[pl.ds(0, PATS - 1)], len_send)
        total = jnp.zeros(BLOCK, F32)
        for q in range(PATS):
            length = jnp.sqrt(jnp.sum(lengths[q], axis=1, keepdims=True))
            total = total + (CLIP / jnp.maximum(length, CLIP)) * pat_slots[q]
        gathered[core, s] = total.astype(BF16)
        wait_blocks(pat_slots.at[pl.ds(0, PATS - 1)], pat_send)


    @pl.when(s < OWNERS)
    def _():
        @pl.loop(1, SLABS)
        def _(q):
            pltpu.make_async_remote_copy(
                gathered.at[core, s], gathered.at[core, s], ag_send, ag_recv,
                device_id=slab_peer(q), device_id_type=MESH,
            ).start()

    wait_owned(gathered.at[0], ag_recv)

    last = pltpu.make_async_remote_copy(
        gathered.at[core], gathered.at[core], core_send, core_recv,
        device_id=(p + 1 - 2 * core, s), device_id_type=MESH,
    )
    last.start()
    last.wait()

    for k in range(2):
        for a in range(3):
            for t in range(LANE_TILES):
                block = gathered[k, a * LANE_TILES + t].astype(F32)
                start = a * ROWS + t % 4 * 128
                if t < 4:
                    out_ref[k, 0:32, start : start + 128] = block
                elif t < 8:
                    out_ref[k, 32:C, start : start + 128] = block
                else:
                    out_ref[k, 0:32, start + 512 : start + ROWS] = block[:, :C]
                    out_ref[k, 32:C, start + 512 : start + ROWS] = block[:, C:]

    @pl.when(s < OWNERS)
    def _():
        wait_blocks(reduced.at[0, pl.ds(0, SLABS - 1)], ag_send)

    for wait in pending:
        wait()


def clipped_gradients(features, cotangent, weights):
    wide = WIDE * CELLS
    vmem, dma = pltpu.VMEM, pltpu.SemaphoreType.DMA
    return pl.pallas_call(
        kernel,
        out_shape=jax.ShapeDtypeStruct((2, C, 3 * ROWS), F32),
        in_specs=[pl.BlockSpec(memory_space=pltpu.HBM)] * 3,
        out_specs=pl.BlockSpec(memory_space=vmem),
        scratch_shapes=[
            vmem((PLANES, C, CELLS), BF16),
            vmem((PLANES, C, CELLS), BF16),
            vmem((2, C, 3 * ROWS), F32),
            vmem((C, wide), BF16),
            vmem((TAPS, 16, CELLS), BF16),
            vmem((2, 3 * C, ROWS), BF16),
            vmem((3 * C, ROWS), BF16),
            vmem((PADDED, wide), BF16),
            vmem((PADDED, wide), BF16),
            vmem((ROWS, wide), BF16),
            vmem((3 * C, wide), F32),
            vmem((C, wide), F32),
            vmem((C, wide), F32),
            vmem((C, wide), F32),
            vmem((3 * C, wide), BF16),
            vmem((3 * C, PADDED), F32),
            vmem((2, C, CELLS), BF16),
            vmem((2, C, CELLS), BF16),
            vmem((2, C, CELLS), F32),
            vmem((2, C, CELLS), F32),
            vmem((5, 1, 128), F32),
            vmem((5, SLABS, 1, 128), F32),
            vmem((2, OWNERS) + BLOCK, BF16),
            vmem((2, SLABS) + BLOCK, BF16),
            vmem((2,) + BLOCK, F32),
            vmem((PATS,) + BLOCK, F32),
            vmem((2, OWNERS) + BLOCK, BF16),
            vmem((PATS, 1, 128), F32),
            dma((4, 2)), dma((4, 2)), dma((5,)), dma((5,)), dma((2,)), dma((2,)), dma, dma, dma, dma, dma, dma, dma, dma, dma((3,)),
        ],
        compiler_params=pltpu.CompilerParams(
            collective_id=0, has_side_effects=True, vmem_limit_bytes=32 * 1024 * 1024
        ),
    )(features, cotangent, weights)


def per_device(features, cotangent, weights, prev_state, tree_noise):
    planes = (features[0].transpose(1, 0, 2), cotangent[0].transpose(1, 0, 2), weights)
    total = clipped_gradients(*(pltpu.with_memory_space_constraint(v, pltpu.HBM) for v in planes))
    return prev_state + total, weights - RATE * (total + tree_noise)


def solution(mesh):
    return jax.shard_map(
        per_device,
        mesh=mesh,
        in_specs=(P("pat", None, "slab", None), P("pat", None, "slab", None), P(), P(), P()),
        out_specs=(P(), P()),
        check_vma=False,
    )
```

```python
import jax
import jax.numpy as jnp
from jax import lax
from jax.experimental import pallas as pl
from jax.experimental.pallas import tpu as pltpu
from jax.sharding import PartitionSpec as P

MESH = pl.DeviceIdType.MESH
C = 64
W = 24
CELLS = 384
PLANES = 6
WIDE = PLANES + 2
TAPS = 9
ROWS = TAPS * C
PADDED = 640
DEEP = 8
TALL = 4
SLABS = TALL * DEEP
PATS = 8
OWNERS = 27
LANE_TILES = 9
BLOCK = (32, 128)
EPS = 1e-05
CLIP = 400.0
RATE = 0.1
COUNT = SLABS * PLANES * CELLS
F32 = jnp.float32
BF16 = jnp.bfloat16


def far_first():
    steps = [(dy, dz) for dy in range(TALL) for dz in range(DEEP) if dy or dz]
    return sorted(steps, key=lambda d: -min(d[0], TALL - d[0]) - min(d[1], DEEP - d[1]))


def sigmoid(v):
    return 1.0 / (1.0 + jnp.exp(-v))


def plane(j, count=1):
    return slice(j * CELLS, (j + count) * CELLS)


def kernel(
    feat_hbm, cot_hbm, w_hbm, noise_hbm, out_ref, stepped_ref,
    feat_ref, cot_ref, w_ref, noise_ref,
    cot, masks, kst, kback, im_feat, im_hid, im_cot, parts, normed_one, normed_two, grad,
    lhs, acc, feat_halo, cot_halo, first_halo, second_halo, rows_out, slots, kg, reduced, scaled, pat_slots, gathered, lengths,
    halo_send, halo_recv, row_send, row_recv, red_send, red_recv, pat_send, pat_recv, len_send, len_recv, deep_send, deep_recv, tall_send, tall_recv, core_send, core_recv, load_sem,
):
    p = lax.axis_index("pat")
    s = lax.axis_index("slab")
    core = lax.rem(p, 2)
    y, z = lax.div(s, DEEP), lax.rem(s, DEEP)

    def peer(dy, dz):
        return (p, lax.rem(y + dy, TALL) * DEEP + lax.rem(z + dz, DEEP))

    slab_peers = [peer(dy, dz) for dy, dz in far_first()]

    def slab_peer(k):
        return (p, lax.rem(s + k, SLABS))

    def pat_peer(k):
        return (lax.rem(p + k, PATS), s)

    pending = []
    barrier = pltpu.get_barrier_semaphore()

    for other in slab_peers:
        pl.semaphore_signal(barrier, inc=1, device_id=other, device_id_type=MESH)

    @pl.loop(1, PATS)
    def _(k):
        pl.semaphore_signal(barrier, inc=1, device_id=pat_peer(k), device_id_type=MESH)

    loads = [
        pltpu.make_async_copy(source, target, load_sem.at[i])
        for i, (source, target) in enumerate(((feat_hbm, feat_ref), (w_hbm, w_ref), (cot_hbm, cot_ref), (noise_hbm, noise_ref)))
    ]
    for load in loads[:2]:
        load.start()

    def halo_copies(stage, low, high, landing):
        return (
            pltpu.make_async_remote_copy(
                low, landing.at[1], halo_send.at[stage, 0], halo_recv.at[stage, 1],
                device_id=slab_peer(SLABS - 1), device_id_type=MESH,
            ),
            pltpu.make_async_remote_copy(
                high, landing.at[0], halo_send.at[stage, 1], halo_recv.at[stage, 0],
                device_id=slab_peer(1), device_id_type=MESH,
            ),
        )

    def wait_blocks(ref, sem):
        pltpu.make_async_copy(ref, ref, sem).wait()

    def wait_owned(ref, sem):
        @pl.when(s < OWNERS)
        def _():
            wait_blocks(ref.at[pl.ds(0, OWNERS - 1)], sem)

        @pl.when(s >= OWNERS)
        def _():
            wait_blocks(ref.at[pl.ds(0, OWNERS)], sem)

    def wait_red(k):
        @pl.when(s < OWNERS)
        def _():
            wait_blocks(reduced.at[k, pl.ds(0, SLABS - 1)], red_recv.at[k])

    def kept(j):
        if 0 < j < WIDE - 1:
            return 1.0
        return jnp.where(s == (0 if j == 0 else SLABS - 1), 0.0, 1.0).astype(F32)

    def eye():
        i = lax.broadcasted_iota(jnp.int32, (128, 128), 0)
        j = lax.broadcasted_iota(jnp.int32, (128, 128), 1)
        return i == j

    def share_row(r, row):
        rows_out[r] = row

        for other in slab_peers:
            pltpu.make_async_remote_copy(
                rows_out.at[r], slots.at[r, s], row_send.at[r], row_recv.at[r],
                device_id=other, device_id_type=MESH,
            ).start()

        slots[r, s] = row
        pending.append(lambda: wait_blocks(slots.at[r, pl.ds(0, SLABS - 1)], row_send.at[r]))

    def row_total(r):
        most = slots.at[r, pl.ds(0, SLABS - 1)]
        pltpu.make_async_copy(most, most, row_recv.at[r]).wait()
        return jnp.sum(slots[r], axis=0)

    def share_pair(r, one, two):
        column = jnp.concatenate([one, two], axis=0)
        share_row(r, jnp.sum(jnp.where(eye(), column, 0.0), axis=0, keepdims=True))

    def pair_total(r):
        row = row_total(r) * (1.0 / COUNT)
        column = jnp.sum(jnp.where(eye(), row, 0.0), axis=1, keepdims=True)
        return column[:C], column[C:]

    def taps(values, im, j):
        for t in range(TAPS):
            shift = (t // 3 - 1) * W + (t % 3 - 1)
            if shift == 0:
                piece = values
            else:
                piece = pltpu.roll(values, (-shift) % CELLS, 1)
                piece = (piece.reshape(C // 16, 16, CELLS) * masks[t]).reshape(C, CELLS)
            im[t * C : (t + 1) * C, plane(j)] = piece

    def multiply(matrix, im, first, count):
        parts[:, plane(first, count)] = jnp.dot(matrix, im[0:ROWS, plane(first, count)], preferred_element_type=F32)

    def combined(j):
        return (
            parts[0:C, plane(j)]
            + parts[C : 2 * C, plane(j + 1)]
            + parts[2 * C : 3 * C, plane(j + 2)]
        )

    def lane_sum(v):
        return v[:, 0:128] + v[:, 128:256] + v[:, 256:384]

    cell = lax.broadcasted_iota(jnp.int32, (16, CELLS), 1)
    row, col = lax.div(cell, W), lax.rem(cell, W)
    for t in range(TAPS):
        b, e = t // 3 - 1, t % 3 - 1
        inside = (row + b >= 0) & (row + b < CELLS // W) & (col + e >= 0) & (col + e < W)
        masks[t] = jnp.where(inside, 1.0, 0.0).astype(BF16)
    loads[1].wait()
    for a in range(3):
        kst[0, a * C : (a + 1) * C, :] = w_ref[0, :, a * ROWS : (a + 1) * ROWS].astype(BF16)
    loads[0].wait()
    for load in loads[2:]:
        load.start()
    for j in range(1, WIDE - 1):
        taps(feat_ref[j - 1], im_feat, j)
    pl.semaphore_wait(barrier, SLABS - 1 + PATS - 1)

    halos = [halo_copies(0, feat_ref.at[0], feat_ref.at[PLANES - 1], feat_halo), halo_copies(1, cot_ref.at[0], cot_ref.at[PLANES - 1], cot_halo)]
    for copy in halos[0]:
        copy.start()
    multiply(kst[0], im_feat, 1, PLANES)
    for copy in halos[0]:
        copy.wait_recv()
        pending.append(copy.wait_send)
    for side, j, a in ((0, 0, 0), (1, WIDE - 1, 2)):
        taps(feat_halo[side] * kept(j).astype(BF16), im_feat, j)
        parts[a * C : (a + 1) * C, plane(j)] = jnp.dot(
            kst[0, a * C : (a + 1) * C, :], im_feat[0:ROWS, plane(j)], preferred_element_type=F32
        )

    def convolved(target, stage, landing):
        one = two = jnp.zeros((C, 128), F32)
        for z in (0, PLANES - 1, 1, 2, 3, 4):
            value = combined(z)
            target[:, plane(z + 1)] = value
            one, two = one + lane_sum(value), two + lane_sum(value * value)
            if z == PLANES - 1:
                pair = halo_copies(stage, target.at[:, plane(1)], target.at[:, plane(PLANES)], landing)
                for copy in pair:
                    copy.start()
        return pair, jnp.sum(one, axis=1, keepdims=True), jnp.sum(two, axis=1, keepdims=True)

    pair, *sums = convolved(normed_one, 2, first_halo)
    share_pair(0, *sums)

    for k in range(2):
        for slot in range(OWNERS, SLABS):
            gathered[k, slot] = jnp.zeros(BLOCK, BF16)
    for load in loads[2:]:
        load.wait()
    stepped_ref[...] = w_ref[...] - RATE * noise_ref[...]
    for a in range(3):
        kst[1, a * C : (a + 1) * C, :] = w_ref[1, :, a * ROWS : (a + 1) * ROWS].astype(BF16)
    turned = jnp.transpose(w_ref[1].astype(BF16).astype(F32))
    for a in range(3):
        for t in range(TAPS):
            block = turned[(a * TAPS + t) * C : (a * TAPS + t + 1) * C, :]
            u = TAPS - 1 - t
            kback[(2 - a) * C : (3 - a) * C, u * C : (u + 1) * C] = block.astype(BF16)
        for j in range(WIDE):
            if not a <= j < a + PLANES:
                lhs[a * C : (a + 1) * C, plane(j)] = jnp.zeros((C, CELLS), BF16)
    for im in (im_feat, im_hid):
        im[ROWS:PADDED, :] = jnp.zeros((PADDED - ROWS, WIDE * CELLS), BF16)

    centre_one, squares = pair_total(0)
    for copy in halos[1]:
        copy.start()
    spread_one = lax.rsqrt(squares - centre_one * centre_one + EPS)
    for copy in pair:
        copy.wait()
    normed_one[:, plane(0)] = first_halo[0]
    normed_one[:, plane(WIDE - 1)] = first_halo[1]

    for j in range(WIDE):
        value = (normed_one[:, plane(j)] - centre_one) * spread_one
        normed_one[:, plane(j)] = value
        taps((value * sigmoid(value) * kept(j)).astype(BF16), im_hid, j)
        if j % 2:
            multiply(kst[1], im_hid, j - 1, 2)

    pair, *sums = convolved(normed_two, 3, second_halo)
    share_pair(1, *sums)
    centre_two, squares = pair_total(1)
    spread_two = lax.rsqrt(squares - centre_two * centre_two + EPS)
    for copy in halos[1]:
        copy.wait()
    for copy in pair:
        copy.wait()
    normed_two[:, plane(0)] = second_halo[0]
    normed_two[:, plane(WIDE - 1)] = second_halo[1]

    def slope(v):
        h = sigmoid(v)
        return h * (1.0 + v * (1.0 - h))

    def second_gradient(j, carry, upstream=None):
        value = (normed_two[:, plane(j)] - centre_two) * spread_two
        normed_two[:, plane(j)] = value
        upstream = cot_ref[j - 1] if upstream is None else upstream
        g = upstream.astype(F32) * slope(value)
        grad[:, plane(j)] = g
        return carry[0] + lane_sum(g), carry[1] + lane_sum(g * value)

    zero = jnp.zeros((C, 128), F32)
    carry = (zero, zero)
    for j in range(1, WIDE - 1):
        carry = second_gradient(j, carry)
    one, two = carry
    share_pair(2, jnp.sum(one, axis=1, keepdims=True), jnp.sum(two, axis=1, keepdims=True))
    second_gradient(0, (zero, zero), cot_halo[0])
    second_gradient(WIDE - 1, (zero, zero), cot_halo[1])
    mean_two, cross_two = pair_total(2)

    for j in range(WIDE):
        value = spread_two * (grad[:, plane(j)] - mean_two - normed_two[:, plane(j)] * cross_two)
        value = (value * kept(j)).astype(BF16)
        cot[:, plane(j)] = value
        taps(value, im_cot, j)
        if j % 2:
            multiply(kback[...], im_cot, j - 1, 2)

    def first_gradient(j, carry):
        value = normed_one[:, plane(j + 1)]
        g = combined(j) * slope(value)
        grad[:, plane(j + 1)] = g
        return carry[0] + lane_sum(g), carry[1] + lane_sum(g * value)

    carry = (zero, zero)
    for j in range(PLANES):
        carry = first_gradient(j, carry)
    one, two = carry
    share_pair(3, jnp.sum(one, axis=1, keepdims=True), jnp.sum(two, axis=1, keepdims=True))

    def kernel_gradient(k, im):
        def send(first, count):
            for a in range(3):
                for t in range(first, first + count):
                    owner = a * LANE_TILES + t

                    @pl.when(s != owner)
                    def _():
                        pltpu.make_async_remote_copy(
                            kg.at[k, owner], reduced.at[k, s], red_send.at[k], red_recv.at[k],
                            device_id=(p, owner), device_id_type=MESH,
                        ).start()

        for first in (0, 256, 512):
            width = 256 if first < 512 else 128
            term = lax.dot_general(
                lhs[...], im[first : first + width, :], (((1,), (1,)), ((), ())), preferred_element_type=F32
            )
            for a in range(3):
                low, high = term[a * C : a * C + 32], term[a * C + 32 : (a + 1) * C]
                if first < 512:
                    for t in range(2):
                        lanes = slice(t * 128, (t + 1) * 128)
                        kg[k, a * LANE_TILES + first // 128 + t] = low[:, lanes].astype(BF16)
                        kg[k, a * LANE_TILES + 4 + first // 128 + t] = high[:, lanes].astype(BF16)
                else:
                    kg[k, a * LANE_TILES + 8] = (low + pltpu.roll(high, C, 1)).astype(BF16)
            if first < 512:
                send(first // 128, 2)
                send(4 + first // 128, 2)
            else:
                send(8, 1)

        @pl.when(s < OWNERS)
        def _():
            reduced[k, s] = kg[k, s]

        pending.append(lambda: wait_owned(kg.at[k], red_send.at[k]))

    def place(j, value):
        for a in range(3):
            lhs[a * C : (a + 1) * C, plane(j + a)] = value

    for j in range(PLANES):
        place(j, cot[:, plane(j + 1)])

    kernel_gradient(1, im_hid)
    mean_one, cross_one = pair_total(3)

    for j in range(PLANES):
        value = spread_one * (grad[:, plane(j + 1)] - mean_one - normed_one[:, plane(j + 1)] * cross_one)
        place(j, value.astype(BF16))

    kernel_gradient(0, im_feat)

    @pl.when(s < OWNERS)
    def _():
        for k in (1, 0):
            wait_red(k)
            scaled[k] = jnp.sum(reduced[k].astype(F32), axis=0)

    @pl.when(s >= OWNERS)
    def _():
        for k in (0, 1):
            scaled[k] = jnp.zeros(BLOCK, F32)

    squared = jnp.sum(scaled[0] * scaled[0] + scaled[1] * scaled[1], axis=0, keepdims=True)
    share_row(4, squared)

    @pl.when(s < OWNERS)
    def _():
        @pl.loop(1, PATS)
        def _(q):
            peer = lax.rem(p + q, PATS)
            pltpu.make_async_remote_copy(
                scaled.at[lax.rem(peer, 2)], pat_slots.at[p], pat_send, pat_recv,
                device_id=(peer, s), device_id_type=MESH,
            ).start()

        pat_slots[p] = scaled[core]

    lengths[p] = row_total(4)

    @pl.when(s < OWNERS)
    def _():
        @pl.loop(1, PATS)
        def _(q):
            pltpu.make_async_remote_copy(
                lengths.at[p], lengths.at[p], len_send, len_recv, device_id=pat_peer(q), device_id_type=MESH
            ).start()

        wait_blocks(pat_slots.at[pl.ds(0, PATS - 1)], pat_recv)
        wait_blocks(lengths.at[pl.ds(0, PATS - 1)], len_recv)
        wait_blocks(lengths.at[pl.ds(0, PATS - 1)], len_send)
        total = jnp.zeros(BLOCK, F32)
        for q in range(PATS):
            length = jnp.sqrt(jnp.sum(lengths[q], axis=1, keepdims=True))
            total = total + (CLIP / jnp.maximum(length, CLIP)) * pat_slots[q]
        gathered[core, s] = total.astype(BF16)
        wait_blocks(pat_slots.at[pl.ds(0, PATS - 1)], pat_send)


    def forward(slot):
        for dy in (2, 1, 3):
            pltpu.make_async_remote_copy(
                gathered.at[core, slot], gathered.at[core, slot], tall_send.at[dy], tall_recv.at[dy],
                device_id=peer(dy, 0), device_id_type=MESH,
            ).start()

    @pl.when(s < OWNERS)
    def _():
        for dz in (4, 3, 5, 2, 6, 1, 7):
            pltpu.make_async_remote_copy(
                gathered.at[core, s], gathered.at[core, s], deep_send.at[dz], deep_recv.at[dz],
                device_id=peer(0, dz), device_id_type=MESH,
            ).start()
        forward(s)

    for dz in (1, 7, 2, 6, 3, 5, 4):
        slot = y * DEEP + lax.rem(z + DEEP - dz, DEEP)

        @pl.when(slot < OWNERS)
        def _():
            wait_blocks(gathered.at[core, slot], deep_recv.at[dz])
            forward(slot)

    def wait_row(owner, sem):
        @pl.when(owner < TALL - 1)
        def _():
            wait_blocks(gathered.at[0, 0:DEEP], sem)

        @pl.when(owner == TALL - 1)
        def _():
            wait_blocks(gathered.at[0, 0 : OWNERS - DEEP * (TALL - 1)], sem)

    def hand_over(dy):
        row = lax.rem(y + TALL - dy, TALL)
        blocks = gathered.at[core, pl.ds(row * DEEP, DEEP)]
        copy = pltpu.make_async_remote_copy(
            blocks, blocks, core_send.at[dy], core_recv.at[dy],
            device_id=(p + 1 - 2 * core, s), device_id_type=MESH,
        )
        copy.start()
        return copy

    rows = [hand_over(0)]
    for dy in (1, 3, 2):
        wait_row(lax.rem(y + TALL - dy, TALL), tall_recv.at[dy])
        rows.append(hand_over(dy))

    def assemble(k):
        for a in range(3):
            for t in range(LANE_TILES):
                block = gathered[k, a * LANE_TILES + t].astype(F32)
                start = a * ROWS + t % 4 * 128
                if t < 4:
                    out_ref[k, 0:32, start : start + 128] = block
                elif t < 8:
                    out_ref[k, 32:C, start : start + 128] = block
                else:
                    out_ref[k, 0:32, start + 512 : start + ROWS] = block[:, :C]
                    out_ref[k, 32:C, start + 512 : start + ROWS] = block[:, C:]

    assemble(core)
    for copy in rows:
        copy.wait()
    assemble(1 - core)

    @pl.when(s < OWNERS)
    def _():
        for dz in range(1, DEEP):
            wait_blocks(gathered.at[0, 0], deep_send.at[dz])

    for dy in range(1, TALL):
        wait_row(y, tall_send.at[dy])
    for wait in pending:
        wait()


def clipped_gradients(features, cotangent, weights, tree_noise):
    wide = WIDE * CELLS
    vmem, dma = pltpu.VMEM, pltpu.SemaphoreType.DMA
    return pl.pallas_call(
        kernel,
        out_shape=[jax.ShapeDtypeStruct((2, C, 3 * ROWS), F32)] * 2,
        in_specs=[pl.BlockSpec(memory_space=pltpu.HBM)] * 4,
        out_specs=[pl.BlockSpec(memory_space=vmem)] * 2,
        scratch_shapes=[
            vmem((PLANES, C, CELLS), BF16),
            vmem((PLANES, C, CELLS), BF16),
            vmem((2, C, 3 * ROWS), F32),
            vmem((2, C, 3 * ROWS), F32),
            vmem((C, wide), BF16),
            vmem((TAPS, 16, CELLS), BF16),
            vmem((2, 3 * C, ROWS), BF16),
            vmem((3 * C, ROWS), BF16),
            vmem((PADDED, wide), BF16),
            vmem((PADDED, wide), BF16),
            vmem((ROWS, wide), BF16),
            vmem((3 * C, wide), F32),
            vmem((C, wide), F32),
            vmem((C, wide), F32),
            vmem((C, wide), F32),
            vmem((3 * C, wide), BF16),
            vmem((3 * C, PADDED), F32),
            vmem((2, C, CELLS), BF16),
            vmem((2, C, CELLS), BF16),
            vmem((2, C, CELLS), F32),
            vmem((2, C, CELLS), F32),
            vmem((5, 1, 128), F32),
            vmem((5, SLABS, 1, 128), F32),
            vmem((2, OWNERS) + BLOCK, BF16),
            vmem((2, SLABS) + BLOCK, BF16),
            vmem((2,) + BLOCK, F32),
            vmem((PATS,) + BLOCK, F32),
            vmem((2, SLABS) + BLOCK, BF16),
            vmem((PATS, 1, 128), F32),
            dma((4, 2)), dma((4, 2)), dma((5,)), dma((5,)), dma((2,)), dma((2,)), dma, dma, dma, dma, dma((DEEP,)), dma((DEEP,)), dma((TALL,)), dma((TALL,)), dma((TALL,)), dma((TALL,)), dma((4,)),
        ],
        compiler_params=pltpu.CompilerParams(
            collective_id=0, has_side_effects=True, vmem_limit_bytes=32 * 1024 * 1024
        ),
    )(features, cotangent, weights, tree_noise)


def per_device(features, cotangent, weights, prev_state, tree_noise):
    planes = (features[0].transpose(1, 0, 2), cotangent[0].transpose(1, 0, 2), weights, tree_noise)
    total, stepped = clipped_gradients(*(pltpu.with_memory_space_constraint(v, pltpu.HBM) for v in planes))
    return prev_state + total, stepped - RATE * total


def solution(mesh):
    return jax.shard_map(
        per_device,
        mesh=mesh,
        in_specs=(P("pat", None, "slab", None), P("pat", None, "slab", None), P(), P(), P()),
        out_specs=(P(), P()),
        check_vma=False,
    )
```

```python
import jax
import jax.numpy as jnp
from jax import lax
from jax.experimental import pallas as pl
from jax.experimental.pallas import tpu as pltpu
from jax.sharding import PartitionSpec as P

MESH = pl.DeviceIdType.MESH
C = 64
W = 24
CELLS = 384
PLANES = 6
WIDE = PLANES + 2
TAPS = 9
ROWS = TAPS * C
PADDED = 640
DEEP = 8
TALL = 4
SLABS = TALL * DEEP
PATS = 8
OWNERS = 27
LANE_TILES = 9
BLOCK = (32, 128)
EPS = 1e-05
CLIP = 400.0
RATE = 0.1
COUNT = SLABS * PLANES * CELLS
F32 = jnp.float32
BF16 = jnp.bfloat16


def far_first():
    steps = [(dy, dz) for dy in range(TALL) for dz in range(DEEP) if dy or dz]
    return sorted(steps, key=lambda d: -min(d[0], TALL - d[0]) - min(d[1], DEEP - d[1]))


def sigmoid(v):
    return 1.0 / (1.0 + jnp.exp(-v))


def plane(j, count=1):
    return slice(j * CELLS, (j + count) * CELLS)


def kernel(
    feat_hbm, cot_hbm, w_hbm, noise_hbm, out_ref, stepped_ref,
    feat_ref, cot_ref, w_ref, noise_ref,
    cot, masks, kst, kback, im_feat, im_hid, im_cot, parts, normed_one, normed_two, grad,
    lhs, acc, feat_halo, cot_halo, feat_far, im_far, far_parts, outer_first, rows_out, slots, kg, reduced, scaled, pat_slots, gathered, lengths,
    halo_send, halo_recv, row_send, row_recv, red_send, red_recv, pat_send, pat_recv, len_send, len_recv, deep_send, deep_recv, tall_send, tall_recv, core_send, core_recv, load_sem,
):
    p = lax.axis_index("pat")
    s = lax.axis_index("slab")
    core = lax.rem(p, 2)
    y, z = lax.div(s, DEEP), lax.rem(s, DEEP)

    def peer(dy, dz):
        return (p, lax.rem(y + dy, TALL) * DEEP + lax.rem(z + dz, DEEP))

    slab_peers = [peer(dy, dz) for dy, dz in far_first()]

    def slab_peer(k):
        return (p, lax.rem(s + k, SLABS))

    def pat_peer(k):
        return (lax.rem(p + k, PATS), s)

    pending = []
    barrier = pltpu.get_barrier_semaphore()

    for other in slab_peers:
        pl.semaphore_signal(barrier, inc=1, device_id=other, device_id_type=MESH)

    @pl.loop(1, PATS)
    def _(k):
        pl.semaphore_signal(barrier, inc=1, device_id=pat_peer(k), device_id_type=MESH)

    loads = [
        pltpu.make_async_copy(source, target, load_sem.at[i])
        for i, (source, target) in enumerate(((feat_hbm, feat_ref), (w_hbm, w_ref), (cot_hbm, cot_ref), (noise_hbm, noise_ref)))
    ]
    for load in loads[:2]:
        load.start()

    def halo_copies(stage, low, high, landing):
        return (
            pltpu.make_async_remote_copy(
                low, landing.at[1], halo_send.at[stage, 0], halo_recv.at[stage, 1],
                device_id=slab_peer(SLABS - 1), device_id_type=MESH,
            ),
            pltpu.make_async_remote_copy(
                high, landing.at[0], halo_send.at[stage, 1], halo_recv.at[stage, 0],
                device_id=slab_peer(1), device_id_type=MESH,
            ),
        )

    def wait_blocks(ref, sem):
        pltpu.make_async_copy(ref, ref, sem).wait()

    def wait_owned(ref, sem):
        @pl.when(s < OWNERS)
        def _():
            wait_blocks(ref.at[pl.ds(0, OWNERS - 1)], sem)

        @pl.when(s >= OWNERS)
        def _():
            wait_blocks(ref.at[pl.ds(0, OWNERS)], sem)

    def wait_red(k):
        @pl.when(s < OWNERS)
        def _():
            wait_blocks(reduced.at[k, pl.ds(0, SLABS - 1)], red_recv.at[k])

    def kept(j):
        if 0 < j < WIDE - 1:
            return 1.0
        return jnp.where(s == (0 if j == 0 else SLABS - 1), 0.0, 1.0).astype(F32)

    def eye():
        i = lax.broadcasted_iota(jnp.int32, (128, 128), 0)
        j = lax.broadcasted_iota(jnp.int32, (128, 128), 1)
        return i == j

    def share_row(r, row):
        rows_out[r] = row

        for other in slab_peers:
            pltpu.make_async_remote_copy(
                rows_out.at[r], slots.at[r, s], row_send.at[r], row_recv.at[r],
                device_id=other, device_id_type=MESH,
            ).start()

        slots[r, s] = row
        pending.append(lambda: wait_blocks(slots.at[r, pl.ds(0, SLABS - 1)], row_send.at[r]))

    def row_total(r):
        most = slots.at[r, pl.ds(0, SLABS - 1)]
        pltpu.make_async_copy(most, most, row_recv.at[r]).wait()
        return jnp.sum(slots[r], axis=0)

    def share_pair(r, one, two):
        column = jnp.concatenate([one, two], axis=0)
        share_row(r, jnp.sum(jnp.where(eye(), column, 0.0), axis=0, keepdims=True))

    def pair_total(r):
        row = row_total(r) * (1.0 / COUNT)
        column = jnp.sum(jnp.where(eye(), row, 0.0), axis=1, keepdims=True)
        return column[:C], column[C:]

    def taps(values, im, j):
        for t in range(TAPS):
            shift = (t // 3 - 1) * W + (t % 3 - 1)
            if shift == 0:
                piece = values
            else:
                piece = pltpu.roll(values, (-shift) % CELLS, 1)
                piece = (piece.reshape(C // 16, 16, CELLS) * masks[t]).reshape(C, CELLS)
            im[t * C : (t + 1) * C, plane(j)] = piece

    def multiply(matrix, im, first, count):
        parts[:, plane(first, count)] = jnp.dot(matrix, im[0:ROWS, plane(first, count)], preferred_element_type=F32)

    def combined(j):
        return (
            parts[0:C, plane(j)]
            + parts[C : 2 * C, plane(j + 1)]
            + parts[2 * C : 3 * C, plane(j + 2)]
        )

    def lane_sum(v):
        return v[:, 0:128] + v[:, 128:256] + v[:, 256:384]

    cell = lax.broadcasted_iota(jnp.int32, (16, CELLS), 1)
    row, col = lax.div(cell, W), lax.rem(cell, W)
    for t in range(TAPS):
        b, e = t // 3 - 1, t % 3 - 1
        inside = (row + b >= 0) & (row + b < CELLS // W) & (col + e >= 0) & (col + e < W)
        masks[t] = jnp.where(inside, 1.0, 0.0).astype(BF16)
    loads[1].wait()
    for a in range(3):
        kst[0, a * C : (a + 1) * C, :] = w_ref[0, :, a * ROWS : (a + 1) * ROWS].astype(BF16)
    loads[0].wait()
    for load in loads[2:]:
        load.start()
    for j in range(1, WIDE - 1):
        taps(feat_ref[j - 1], im_feat, j)
    pl.semaphore_wait(barrier, SLABS - 1 + PATS - 1)

    halos = [halo_copies(0, feat_ref.at[0], feat_ref.at[PLANES - 1], feat_halo), halo_copies(1, cot_ref.at[0], cot_ref.at[PLANES - 1], cot_halo),
        halo_copies(2, feat_ref.at[1:3], feat_ref.at[3:5], feat_far)]
    for pair in (halos[0], halos[2]):
        for copy in pair:
            copy.start()
    multiply(kst[0], im_feat, 1, PLANES)
    for copy in halos[0]:
        copy.wait_recv()
        pending.append(copy.wait_send)
    for side, j, a in ((0, 0, 0), (1, WIDE - 1, 2)):
        taps(feat_halo[side] * kept(j).astype(BF16), im_feat, j)
        parts[a * C : (a + 1) * C, plane(j)] = jnp.dot(
            kst[0, a * C : (a + 1) * C, :], im_feat[0:ROWS, plane(j)], preferred_element_type=F32
        )

    def convolved(target):
        one = two = jnp.zeros((C, 128), F32)
        for z in range(PLANES):
            value = combined(z)
            target[:, plane(z + 1)] = value
            one, two = one + lane_sum(value), two + lane_sum(value * value)
        return jnp.sum(one, axis=1, keepdims=True), jnp.sum(two, axis=1, keepdims=True)

    share_pair(0, *convolved(normed_one))

    for k in range(2):
        for slot in range(OWNERS, SLABS):
            gathered[k, slot] = jnp.zeros(BLOCK, BF16)
    for load in loads[2:]:
        load.wait()
    stepped_ref[...] = w_ref[...] - RATE * noise_ref[...]
    for a in range(3):
        kst[1, a * C : (a + 1) * C, :] = w_ref[1, :, a * ROWS : (a + 1) * ROWS].astype(BF16)
    turned = jnp.transpose(w_ref[1].astype(BF16).astype(F32))
    for a in range(3):
        for t in range(TAPS):
            block = turned[(a * TAPS + t) * C : (a * TAPS + t + 1) * C, :]
            u = TAPS - 1 - t
            kback[(2 - a) * C : (3 - a) * C, u * C : (u + 1) * C] = block.astype(BF16)
        for j in range(WIDE):
            if not a <= j < a + PLANES:
                lhs[a * C : (a + 1) * C, plane(j)] = jnp.zeros((C, CELLS), BF16)
    for im in (im_feat, im_hid):
        im[ROWS:PADDED, :] = jnp.zeros((PADDED - ROWS, WIDE * CELLS), BF16)

    parts[C : 3 * C, plane(0)] = jnp.dot(kst[0, C : 3 * C, :], im_feat[0:ROWS, plane(0)], preferred_element_type=F32)
    parts[0 : 2 * C, plane(WIDE - 1)] = jnp.dot(
        kst[0, 0 : 2 * C, :], im_feat[0:ROWS, plane(WIDE - 1)], preferred_element_type=F32
    )
    for copy in halos[2]:
        copy.wait()
    for i in range(4):
        taps(feat_far[i // 2, i % 2], im_far, i)
    far_parts[...] = jnp.dot(kst[0], im_far[...], preferred_element_type=F32)
    low, mid, high = slice(0, C), slice(C, 2 * C), slice(2 * C, 3 * C)
    normed_one[:, plane(0)] = far_parts[low, plane(1)] + parts[mid, plane(0)] + parts[high, plane(1)]
    normed_one[:, plane(WIDE - 1)] = parts[low, plane(6)] + parts[mid, plane(7)] + far_parts[high, plane(2)]
    outer_first[:, plane(0)] = far_parts[low, plane(0)] + far_parts[mid, plane(1)] + parts[high, plane(0)]
    outer_first[:, plane(1)] = parts[low, plane(7)] + far_parts[mid, plane(2)] + far_parts[high, plane(3)]

    centre_one, squares = pair_total(0)
    for copy in halos[1]:
        copy.start()
    spread_one = lax.rsqrt(squares - centre_one * centre_one + EPS)
    for j in range(WIDE):
        value = (normed_one[:, plane(j)] - centre_one) * spread_one
        normed_one[:, plane(j)] = value
        taps((value * sigmoid(value) * kept(j)).astype(BF16), im_hid, j)
        if j % 2:
            multiply(kst[1], im_hid, j - 1, 2)

    share_pair(1, *convolved(normed_two))
    for i, j, a in ((0, 0, low), (1, WIDE - 1, high)):
        value = (outer_first[:, plane(i)] - centre_one) * spread_one
        taps((value * sigmoid(value) * kept(j)).astype(BF16), im_far, i)
        far_parts[a, plane(i)] = jnp.dot(kst[1, a, :], im_far[:, plane(i)], preferred_element_type=F32)
    normed_two[:, plane(0)] = far_parts[low, plane(0)] + parts[mid, plane(0)] + parts[high, plane(1)]
    normed_two[:, plane(WIDE - 1)] = parts[low, plane(6)] + parts[mid, plane(7)] + far_parts[high, plane(1)]
    centre_two, squares = pair_total(1)
    spread_two = lax.rsqrt(squares - centre_two * centre_two + EPS)
    for copy in halos[1]:
        copy.wait()
    def slope(v):
        h = sigmoid(v)
        return h * (1.0 + v * (1.0 - h))

    def second_gradient(j, carry, upstream=None):
        value = (normed_two[:, plane(j)] - centre_two) * spread_two
        normed_two[:, plane(j)] = value
        upstream = cot_ref[j - 1] if upstream is None else upstream
        g = upstream.astype(F32) * slope(value)
        grad[:, plane(j)] = g
        return carry[0] + lane_sum(g), carry[1] + lane_sum(g * value)

    zero = jnp.zeros((C, 128), F32)
    carry = (zero, zero)
    for j in range(1, WIDE - 1):
        carry = second_gradient(j, carry)
    one, two = carry
    share_pair(2, jnp.sum(one, axis=1, keepdims=True), jnp.sum(two, axis=1, keepdims=True))
    second_gradient(0, (zero, zero), cot_halo[0])
    second_gradient(WIDE - 1, (zero, zero), cot_halo[1])
    mean_two, cross_two = pair_total(2)

    for j in range(WIDE):
        value = spread_two * (grad[:, plane(j)] - mean_two - normed_two[:, plane(j)] * cross_two)
        value = (value * kept(j)).astype(BF16)
        cot[:, plane(j)] = value
        taps(value, im_cot, j)
        if j % 2:
            multiply(kback[...], im_cot, j - 1, 2)

    def first_gradient(j, carry):
        value = normed_one[:, plane(j + 1)]
        g = combined(j) * slope(value)
        grad[:, plane(j + 1)] = g
        return carry[0] + lane_sum(g), carry[1] + lane_sum(g * value)

    carry = (zero, zero)
    for j in range(PLANES):
        carry = first_gradient(j, carry)
    one, two = carry
    share_pair(3, jnp.sum(one, axis=1, keepdims=True), jnp.sum(two, axis=1, keepdims=True))

    def kernel_gradient(k, im):
        def send(first, count):
            for a in range(3):
                for t in range(first, first + count):
                    owner = a * LANE_TILES + t

                    @pl.when(s != owner)
                    def _():
                        pltpu.make_async_remote_copy(
                            kg.at[k, owner], reduced.at[k, s], red_send.at[k], red_recv.at[k],
                            device_id=(p, owner), device_id_type=MESH,
                        ).start()

        for first in (0, 256, 512):
            width = 256 if first < 512 else 128
            term = lax.dot_general(
                lhs[...], im[first : first + width, :], (((1,), (1,)), ((), ())), preferred_element_type=F32
            )
            for a in range(3):
                low, high = term[a * C : a * C + 32], term[a * C + 32 : (a + 1) * C]
                if first < 512:
                    for t in range(2):
                        lanes = slice(t * 128, (t + 1) * 128)
                        kg[k, a * LANE_TILES + first // 128 + t] = low[:, lanes].astype(BF16)
                        kg[k, a * LANE_TILES + 4 + first // 128 + t] = high[:, lanes].astype(BF16)
                else:
                    kg[k, a * LANE_TILES + 8] = (low + pltpu.roll(high, C, 1)).astype(BF16)
            if first < 512:
                send(first // 128, 2)
                send(4 + first // 128, 2)
            else:
                send(8, 1)

        @pl.when(s < OWNERS)
        def _():
            reduced[k, s] = kg[k, s]

        pending.append(lambda: wait_owned(kg.at[k], red_send.at[k]))

    def place(j, value):
        for a in range(3):
            lhs[a * C : (a + 1) * C, plane(j + a)] = value

    for j in range(PLANES):
        place(j, cot[:, plane(j + 1)])

    kernel_gradient(1, im_hid)
    mean_one, cross_one = pair_total(3)

    for j in range(PLANES):
        value = spread_one * (grad[:, plane(j + 1)] - mean_one - normed_one[:, plane(j + 1)] * cross_one)
        place(j, value.astype(BF16))

    kernel_gradient(0, im_feat)

    @pl.when(s < OWNERS)
    def _():
        for k in (1, 0):
            wait_red(k)
            scaled[k] = jnp.sum(reduced[k].astype(F32), axis=0)

    @pl.when(s >= OWNERS)
    def _():
        for k in (0, 1):
            scaled[k] = jnp.zeros(BLOCK, F32)

    squared = jnp.sum(scaled[0] * scaled[0] + scaled[1] * scaled[1], axis=0, keepdims=True)
    share_row(4, squared)

    @pl.when(s < OWNERS)
    def _():
        @pl.loop(1, PATS)
        def _(q):
            peer = lax.rem(p + q, PATS)
            pltpu.make_async_remote_copy(
                scaled.at[lax.rem(peer, 2)], pat_slots.at[p], pat_send, pat_recv,
                device_id=(peer, s), device_id_type=MESH,
            ).start()

        pat_slots[p] = scaled[core]

    lengths[p] = row_total(4)

    @pl.when(s < OWNERS)
    def _():
        @pl.loop(1, PATS)
        def _(q):
            pltpu.make_async_remote_copy(
                lengths.at[p], lengths.at[p], len_send, len_recv, device_id=pat_peer(q), device_id_type=MESH
            ).start()

        wait_blocks(pat_slots.at[pl.ds(0, PATS - 1)], pat_recv)
        wait_blocks(lengths.at[pl.ds(0, PATS - 1)], len_recv)
        wait_blocks(lengths.at[pl.ds(0, PATS - 1)], len_send)
        total = jnp.zeros(BLOCK, F32)
        for q in range(PATS):
            length = jnp.sqrt(jnp.sum(lengths[q], axis=1, keepdims=True))
            total = total + (CLIP / jnp.maximum(length, CLIP)) * pat_slots[q]
        gathered[core, s] = total.astype(BF16)
        wait_blocks(pat_slots.at[pl.ds(0, PATS - 1)], pat_send)


    def forward(slot):
        for dy in (2, 1, 3):
            pltpu.make_async_remote_copy(
                gathered.at[core, slot], gathered.at[core, slot], tall_send.at[dy], tall_recv.at[dy],
                device_id=peer(dy, 0), device_id_type=MESH,
            ).start()

    @pl.when(s < OWNERS)
    def _():
        for dz in (4, 3, 5, 2, 6, 1, 7):
            pltpu.make_async_remote_copy(
                gathered.at[core, s], gathered.at[core, s], deep_send.at[dz], deep_recv.at[dz],
                device_id=peer(0, dz), device_id_type=MESH,
            ).start()
        forward(s)

    for dz in (1, 7, 2, 6, 3, 5, 4):
        slot = y * DEEP + lax.rem(z + DEEP - dz, DEEP)

        @pl.when(slot < OWNERS)
        def _():
            wait_blocks(gathered.at[core, slot], deep_recv.at[dz])
            forward(slot)

    def wait_row(owner, sem):
        @pl.when(owner < TALL - 1)
        def _():
            wait_blocks(gathered.at[0, 0:DEEP], sem)

        @pl.when(owner == TALL - 1)
        def _():
            wait_blocks(gathered.at[0, 0 : OWNERS - DEEP * (TALL - 1)], sem)

    def hand_over(dy):
        row = lax.rem(y + TALL - dy, TALL)
        blocks = gathered.at[core, pl.ds(row * DEEP, DEEP)]
        copy = pltpu.make_async_remote_copy(
            blocks, blocks, core_send.at[dy], core_recv.at[dy],
            device_id=(p + 1 - 2 * core, s), device_id_type=MESH,
        )
        copy.start()
        return copy

    rows = [hand_over(0)]
    for dy in (1, 3, 2):
        wait_row(lax.rem(y + TALL - dy, TALL), tall_recv.at[dy])
        rows.append(hand_over(dy))

    def assemble(k):
        for a in range(3):
            for t in range(LANE_TILES):
                block = gathered[k, a * LANE_TILES + t].astype(F32)
                start = a * ROWS + t % 4 * 128
                if t < 4:
                    out_ref[k, 0:32, start : start + 128] = block
                elif t < 8:
                    out_ref[k, 32:C, start : start + 128] = block
                else:
                    out_ref[k, 0:32, start + 512 : start + ROWS] = block[:, :C]
                    out_ref[k, 32:C, start + 512 : start + ROWS] = block[:, C:]

    assemble(core)
    for copy in rows:
        copy.wait()
    assemble(1 - core)

    @pl.when(s < OWNERS)
    def _():
        for dz in range(1, DEEP):
            wait_blocks(gathered.at[0, 0], deep_send.at[dz])

    for dy in range(1, TALL):
        wait_row(y, tall_send.at[dy])
    for wait in pending:
        wait()


def clipped_gradients(features, cotangent, weights, tree_noise):
    wide = WIDE * CELLS
    vmem, dma = pltpu.VMEM, pltpu.SemaphoreType.DMA
    return pl.pallas_call(
        kernel,
        out_shape=[jax.ShapeDtypeStruct((2, C, 3 * ROWS), F32)] * 2,
        in_specs=[pl.BlockSpec(memory_space=pltpu.HBM)] * 4,
        out_specs=[pl.BlockSpec(memory_space=vmem)] * 2,
        scratch_shapes=[
            vmem((PLANES, C, CELLS), BF16),
            vmem((PLANES, C, CELLS), BF16),
            vmem((2, C, 3 * ROWS), F32),
            vmem((2, C, 3 * ROWS), F32),
            vmem((C, wide), BF16),
            vmem((TAPS, 16, CELLS), BF16),
            vmem((2, 3 * C, ROWS), BF16),
            vmem((3 * C, ROWS), BF16),
            vmem((PADDED, wide), BF16),
            vmem((PADDED, wide), BF16),
            vmem((ROWS, wide), BF16),
            vmem((3 * C, wide), F32),
            vmem((C, wide), F32),
            vmem((C, wide), F32),
            vmem((C, wide), F32),
            vmem((3 * C, wide), BF16),
            vmem((3 * C, PADDED), F32),
            vmem((2, C, CELLS), BF16),
            vmem((2, C, CELLS), BF16),
            vmem((2, 2, C, CELLS), BF16),
            vmem((ROWS, 4 * CELLS), BF16),
            vmem((3 * C, 4 * CELLS), F32),
            vmem((C, 2 * CELLS), F32),
            vmem((5, 1, 128), F32),
            vmem((5, SLABS, 1, 128), F32),
            vmem((2, OWNERS) + BLOCK, BF16),
            vmem((2, SLABS) + BLOCK, BF16),
            vmem((2,) + BLOCK, F32),
            vmem((PATS,) + BLOCK, F32),
            vmem((2, SLABS) + BLOCK, BF16),
            vmem((PATS, 1, 128), F32),
            dma((3, 2)), dma((3, 2)), dma((5,)), dma((5,)), dma((2,)), dma((2,)), dma, dma, dma, dma, dma((DEEP,)), dma((DEEP,)), dma((TALL,)), dma((TALL,)), dma((TALL,)), dma((TALL,)), dma((4,)),
        ],
        compiler_params=pltpu.CompilerParams(
            collective_id=0, has_side_effects=True, vmem_limit_bytes=32 * 1024 * 1024
        ),
    )(features, cotangent, weights, tree_noise)


def per_device(features, cotangent, weights, prev_state, tree_noise):
    planes = (features[0].transpose(1, 0, 2), cotangent[0].transpose(1, 0, 2), weights, tree_noise)
    total, stepped = clipped_gradients(*(pltpu.with_memory_space_constraint(v, pltpu.HBM) for v in planes))
    return prev_state + total, stepped - RATE * total


def solution(mesh):
    return jax.shard_map(
        per_device,
        mesh=mesh,
        in_specs=(P("pat", None, "slab", None), P("pat", None, "slab", None), P(), P(), P()),
        out_specs=(P(), P()),
        check_vma=False,
    )
```

```python
import jax
import jax.numpy as jnp
from jax import lax
from jax.experimental import pallas as pl
from jax.experimental.pallas import tpu as pltpu
from jax.sharding import PartitionSpec as P

MESH = pl.DeviceIdType.MESH
C = 64
W = 24
CELLS = 384
PLANES = 6
WIDE = PLANES + 2
TAPS = 9
ROWS = TAPS * C
PADDED = 640
DEEP = 8
TALL = 4
SLABS = TALL * DEEP
PATS = 8
OWNERS = 27
LANE_TILES = 9
BLOCK = (32, 128)
EPS = 1e-05
CLIP = 400.0
RATE = 0.1
COUNT = SLABS * PLANES * CELLS
F32 = jnp.float32
BF16 = jnp.bfloat16


def far_first():
    steps = [(dy, dz) for dy in range(TALL) for dz in range(DEEP) if dy or dz]
    return sorted(steps, key=lambda d: -min(d[0], TALL - d[0]) - min(d[1], DEEP - d[1]))


def sigmoid(v):
    return 1.0 / (1.0 + jnp.exp(-v))


def plane(j, count=1):
    return slice(j * CELLS, (j + count) * CELLS)


def kernel(
    feat_hbm, cot_hbm, w_hbm, noise_hbm, out_ref, stepped_ref,
    feat_ref, cot_ref, w_ref, noise_ref,
    cot, masks, kst, kback, im_feat, im_hid, im_cot, parts, normed_one, normed_two, grad,
    lhs, acc, feat_halo, cot_halo, feat_far, im_far, far_parts, outer_first, slope_one, rows_out, slots, kg, reduced, scaled, pat_slots, gathered, lengths,
    halo_send, halo_recv, row_send, row_recv, red_send, red_recv, pat_send, pat_recv, len_send, len_recv, deep_send, deep_recv, tall_send, tall_recv, core_send, core_recv, load_sem,
):
    p = lax.axis_index("pat")
    s = lax.axis_index("slab")
    core = lax.rem(p, 2)
    y, z = lax.div(s, DEEP), lax.rem(s, DEEP)

    def peer(dy, dz):
        return (p, lax.rem(y + dy, TALL) * DEEP + lax.rem(z + dz, DEEP))

    slab_peers = [peer(dy, dz) for dy, dz in far_first()]

    def slab_peer(k):
        return (p, lax.rem(s + k, SLABS))

    def pat_peer(k):
        return (lax.rem(p + k, PATS), s)

    pending = []
    barrier = pltpu.get_barrier_semaphore()

    for other in slab_peers:
        pl.semaphore_signal(barrier, inc=1, device_id=other, device_id_type=MESH)

    @pl.loop(1, PATS)
    def _(k):
        pl.semaphore_signal(barrier, inc=1, device_id=pat_peer(k), device_id_type=MESH)

    loads = [
        pltpu.make_async_copy(source, target, load_sem.at[i])
        for i, (source, target) in enumerate(((feat_hbm, feat_ref), (w_hbm, w_ref), (cot_hbm, cot_ref), (noise_hbm, noise_ref)))
    ]
    for load in loads[:2]:
        load.start()

    def halo_copies(stage, low, high, landing):
        return (
            pltpu.make_async_remote_copy(
                low, landing.at[1], halo_send.at[stage, 0], halo_recv.at[stage, 1],
                device_id=slab_peer(SLABS - 1), device_id_type=MESH,
            ),
            pltpu.make_async_remote_copy(
                high, landing.at[0], halo_send.at[stage, 1], halo_recv.at[stage, 0],
                device_id=slab_peer(1), device_id_type=MESH,
            ),
        )

    def wait_blocks(ref, sem):
        pltpu.make_async_copy(ref, ref, sem).wait()

    def wait_owned(ref, sem):
        @pl.when(s < OWNERS)
        def _():
            wait_blocks(ref.at[pl.ds(0, OWNERS - 1)], sem)

        @pl.when(s >= OWNERS)
        def _():
            wait_blocks(ref.at[pl.ds(0, OWNERS)], sem)

    def wait_red(k):
        @pl.when(s < OWNERS)
        def _():
            wait_blocks(reduced.at[k, pl.ds(0, SLABS - 1)], red_recv.at[k])

    def kept(j):
        if 0 < j < WIDE - 1:
            return 1.0
        return jnp.where(s == (0 if j == 0 else SLABS - 1), 0.0, 1.0).astype(F32)

    def eye():
        i = lax.broadcasted_iota(jnp.int32, (128, 128), 0)
        j = lax.broadcasted_iota(jnp.int32, (128, 128), 1)
        return i == j

    def share_row(r, row):
        rows_out[r] = row

        for other in slab_peers:
            pltpu.make_async_remote_copy(
                rows_out.at[r], slots.at[r, s], row_send.at[r], row_recv.at[r],
                device_id=other, device_id_type=MESH,
            ).start()

        slots[r, s] = row
        pending.append(lambda: wait_blocks(slots.at[r, pl.ds(0, SLABS - 1)], row_send.at[r]))

    def row_total(r):
        most = slots.at[r, pl.ds(0, SLABS - 1)]
        pltpu.make_async_copy(most, most, row_recv.at[r]).wait()
        return jnp.sum(slots[r], axis=0)

    def share_pair(r, one, two):
        lanes = jnp.transpose(jnp.concatenate([one, two], axis=0))
        share_row(r, jnp.sum(lanes, axis=0, keepdims=True))

    def pair_total(r):
        row = row_total(r) * (1.0 / COUNT)
        column = jnp.sum(jnp.where(eye(), row, 0.0), axis=1, keepdims=True)
        return column[:C], column[C:]

    def taps(values, im, j):
        for t in range(TAPS):
            shift = (t // 3 - 1) * W + (t % 3 - 1)
            if shift == 0:
                piece = values
            else:
                piece = pltpu.roll(values, (-shift) % CELLS, 1)
                piece = (piece.reshape(C // 16, 16, CELLS) * masks[t]).reshape(C, CELLS)
            im[t * C : (t + 1) * C, plane(j)] = piece

    def multiply(matrix, im, first, count):
        parts[:, plane(first, count)] = jnp.dot(matrix, im[0:ROWS, plane(first, count)], preferred_element_type=F32)

    def combined(j):
        return (
            parts[0:C, plane(j)]
            + parts[C : 2 * C, plane(j + 1)]
            + parts[2 * C : 3 * C, plane(j + 2)]
        )

    def lane_sum(v):
        return v[:, 0:128] + v[:, 128:256] + v[:, 256:384]

    cell = lax.broadcasted_iota(jnp.int32, (16, CELLS), 1)
    row, col = lax.div(cell, W), lax.rem(cell, W)
    for t in range(TAPS):
        b, e = t // 3 - 1, t % 3 - 1
        inside = (row + b >= 0) & (row + b < CELLS // W) & (col + e >= 0) & (col + e < W)
        masks[t] = jnp.where(inside, 1.0, 0.0).astype(BF16)
    loads[1].wait()
    for a in range(3):
        kst[0, a * C : (a + 1) * C, :] = w_ref[0, :, a * ROWS : (a + 1) * ROWS].astype(BF16)
    loads[0].wait()
    for load in loads[2:]:
        load.start()
    for j in range(1, WIDE - 1):
        taps(feat_ref[j - 1], im_feat, j)
    pl.semaphore_wait(barrier, SLABS - 1 + PATS - 1)

    halos = [halo_copies(0, feat_ref.at[0], feat_ref.at[PLANES - 1], feat_halo), halo_copies(1, cot_ref.at[0], cot_ref.at[PLANES - 1], cot_halo),
        halo_copies(2, feat_ref.at[1:3], feat_ref.at[3:5], feat_far)]
    for pair in (halos[0], halos[2]):
        for copy in pair:
            copy.start()
    multiply(kst[0], im_feat, 1, PLANES)
    for copy in halos[0]:
        copy.wait_recv()
        pending.append(copy.wait_send)
    for side, j, a in ((0, 0, 0), (1, WIDE - 1, 2)):
        taps(feat_halo[side] * kept(j).astype(BF16), im_feat, j)
        parts[a * C : (a + 1) * C, plane(j)] = jnp.dot(
            kst[0, a * C : (a + 1) * C, :], im_feat[0:ROWS, plane(j)], preferred_element_type=F32
        )

    def convolved(target):
        one = two = jnp.zeros((C, 128), F32)
        for z in range(PLANES):
            value = combined(z)
            target[:, plane(z + 1)] = value
            one, two = one + lane_sum(value), two + lane_sum(value * value)
        return one, two

    share_pair(0, *convolved(normed_one))

    for k in range(2):
        for slot in range(OWNERS, SLABS):
            gathered[k, slot] = jnp.zeros(BLOCK, BF16)
    for load in loads[2:]:
        load.wait()
    stepped_ref[...] = w_ref[...] - RATE * noise_ref[...]
    for a in range(3):
        kst[1, a * C : (a + 1) * C, :] = w_ref[1, :, a * ROWS : (a + 1) * ROWS].astype(BF16)
    turned = jnp.transpose(w_ref[1].astype(BF16).astype(F32))
    for a in range(3):
        for t in range(TAPS):
            block = turned[(a * TAPS + t) * C : (a * TAPS + t + 1) * C, :]
            u = TAPS - 1 - t
            kback[(2 - a) * C : (3 - a) * C, u * C : (u + 1) * C] = block.astype(BF16)
        for j in range(WIDE):
            if not a <= j < a + PLANES:
                lhs[a * C : (a + 1) * C, plane(j)] = jnp.zeros((C, CELLS), BF16)
    for im in (im_feat, im_hid):
        im[ROWS:PADDED, :] = jnp.zeros((PADDED - ROWS, WIDE * CELLS), BF16)

    parts[C : 3 * C, plane(0)] = jnp.dot(kst[0, C : 3 * C, :], im_feat[0:ROWS, plane(0)], preferred_element_type=F32)
    parts[0 : 2 * C, plane(WIDE - 1)] = jnp.dot(
        kst[0, 0 : 2 * C, :], im_feat[0:ROWS, plane(WIDE - 1)], preferred_element_type=F32
    )
    for copy in halos[2]:
        copy.wait()
    for i in range(4):
        taps(feat_far[i // 2, i % 2], im_far, i)
    far_parts[...] = jnp.dot(kst[0], im_far[...], preferred_element_type=F32)
    low, mid, high = slice(0, C), slice(C, 2 * C), slice(2 * C, 3 * C)
    normed_one[:, plane(0)] = far_parts[low, plane(1)] + parts[mid, plane(0)] + parts[high, plane(1)]
    normed_one[:, plane(WIDE - 1)] = parts[low, plane(6)] + parts[mid, plane(7)] + far_parts[high, plane(2)]
    outer_first[:, plane(0)] = far_parts[low, plane(0)] + far_parts[mid, plane(1)] + parts[high, plane(0)]
    outer_first[:, plane(1)] = parts[low, plane(7)] + far_parts[mid, plane(2)] + far_parts[high, plane(3)]

    centre_one, squares = pair_total(0)
    for copy in halos[1]:
        copy.start()
    spread_one = lax.rsqrt(squares - centre_one * centre_one + EPS)
    for j in range(WIDE):
        value = (normed_one[:, plane(j)] - centre_one) * spread_one
        normed_one[:, plane(j)] = value
        taps((value * sigmoid(value) * kept(j)).astype(BF16), im_hid, j)
        if j % 2:
            multiply(kst[1], im_hid, j - 1, 2)

    def slope(v):
        h = sigmoid(v)
        return h * (1.0 + v * (1.0 - h))

    share_pair(1, *convolved(normed_two))
    for i, j, a in ((0, 0, low), (1, WIDE - 1, high)):
        value = (outer_first[:, plane(i)] - centre_one) * spread_one
        taps((value * sigmoid(value) * kept(j)).astype(BF16), im_far, i)
        far_parts[a, plane(i)] = jnp.dot(kst[1, a, :], im_far[:, plane(i)], preferred_element_type=F32)
    normed_two[:, plane(0)] = far_parts[low, plane(0)] + parts[mid, plane(0)] + parts[high, plane(1)]
    normed_two[:, plane(WIDE - 1)] = parts[low, plane(6)] + parts[mid, plane(7)] + far_parts[high, plane(1)]
    centre_two, squares = pair_total(1)
    spread_two = lax.rsqrt(squares - centre_two * centre_two + EPS)
    for copy in halos[1]:
        copy.wait()
    def second_gradient(j, carry, upstream=None):
        value = (normed_two[:, plane(j)] - centre_two) * spread_two
        normed_two[:, plane(j)] = value
        upstream = cot_ref[j - 1] if upstream is None else upstream
        g = upstream.astype(F32) * slope(value)
        grad[:, plane(j)] = g
        return carry[0] + lane_sum(g), carry[1] + lane_sum(g * value)

    zero = jnp.zeros((C, 128), F32)
    carry = (zero, zero)
    for j in range(1, WIDE - 1):
        carry = second_gradient(j, carry)
    one, two = carry
    share_pair(2, one, two)
    second_gradient(0, (zero, zero), cot_halo[0])
    second_gradient(WIDE - 1, (zero, zero), cot_halo[1])
    for j in range(1, WIDE - 1):
        slope_one[:, plane(j)] = slope(normed_one[:, plane(j)])
    mean_two, cross_two = pair_total(2)

    for j in range(WIDE):
        value = spread_two * (grad[:, plane(j)] - mean_two - normed_two[:, plane(j)] * cross_two)
        value = (value * kept(j)).astype(BF16)
        cot[:, plane(j)] = value
        taps(value, im_cot, j)
        if j % 2:
            multiply(kback[...], im_cot, j - 1, 2)

    def first_gradient(j, carry):
        value = normed_one[:, plane(j + 1)]
        g = combined(j) * slope_one[:, plane(j + 1)]
        grad[:, plane(j + 1)] = g
        return carry[0] + lane_sum(g), carry[1] + lane_sum(g * value)

    carry = (zero, zero)
    for j in range(PLANES):
        carry = first_gradient(j, carry)
    one, two = carry
    share_pair(3, one, two)

    def kernel_gradient(k, im):
        def send(first, count):
            for a in range(3):
                for t in range(first, first + count):
                    owner = a * LANE_TILES + t

                    @pl.when(s != owner)
                    def _():
                        pltpu.make_async_remote_copy(
                            kg.at[k, owner], reduced.at[k, s], red_send.at[k], red_recv.at[k],
                            device_id=(p, owner), device_id_type=MESH,
                        ).start()

        for first in (0, 256, 512):
            width = 256 if first < 512 else 128
            term = lax.dot_general(
                lhs[...], im[first : first + width, :], (((1,), (1,)), ((), ())), preferred_element_type=F32
            )
            for a in range(3):
                low, high = term[a * C : a * C + 32], term[a * C + 32 : (a + 1) * C]
                if first < 512:
                    for t in range(2):
                        lanes = slice(t * 128, (t + 1) * 128)
                        kg[k, a * LANE_TILES + first // 128 + t] = low[:, lanes].astype(BF16)
                        kg[k, a * LANE_TILES + 4 + first // 128 + t] = high[:, lanes].astype(BF16)
                else:
                    kg[k, a * LANE_TILES + 8] = (low + pltpu.roll(high, C, 1)).astype(BF16)
            if first < 512:
                send(first // 128, 2)
                send(4 + first // 128, 2)
            else:
                send(8, 1)

        @pl.when(s < OWNERS)
        def _():
            reduced[k, s] = kg[k, s]

        pending.append(lambda: wait_owned(kg.at[k], red_send.at[k]))

    def place(j, value):
        for a in range(3):
            lhs[a * C : (a + 1) * C, plane(j + a)] = value

    for j in range(PLANES):
        place(j, cot[:, plane(j + 1)])

    kernel_gradient(1, im_hid)
    mean_one, cross_one = pair_total(3)

    for j in range(PLANES):
        value = spread_one * (grad[:, plane(j + 1)] - mean_one - normed_one[:, plane(j + 1)] * cross_one)
        place(j, value.astype(BF16))

    kernel_gradient(0, im_feat)

    @pl.when(s < OWNERS)
    def _():
        for k in (1, 0):
            wait_red(k)
            scaled[k] = jnp.sum(reduced[k].astype(F32), axis=0)

    @pl.when(s >= OWNERS)
    def _():
        for k in (0, 1):
            scaled[k] = jnp.zeros(BLOCK, F32)

    squared = jnp.sum(scaled[0] * scaled[0] + scaled[1] * scaled[1], axis=0, keepdims=True)
    share_row(4, squared)

    @pl.when(s < OWNERS)
    def _():
        @pl.loop(1, PATS)
        def _(q):
            peer = lax.rem(p + q, PATS)
            pltpu.make_async_remote_copy(
                scaled.at[lax.rem(peer, 2)], pat_slots.at[p], pat_send, pat_recv,
                device_id=(peer, s), device_id_type=MESH,
            ).start()

        pat_slots[p] = scaled[core]

    lengths[p] = row_total(4)

    @pl.when(s < OWNERS)
    def _():
        @pl.loop(1, PATS)
        def _(q):
            pltpu.make_async_remote_copy(
                lengths.at[p], lengths.at[p], len_send, len_recv, device_id=pat_peer(q), device_id_type=MESH
            ).start()

        wait_blocks(pat_slots.at[pl.ds(0, PATS - 1)], pat_recv)
        wait_blocks(lengths.at[pl.ds(0, PATS - 1)], len_recv)
        wait_blocks(lengths.at[pl.ds(0, PATS - 1)], len_send)
        total = jnp.zeros(BLOCK, F32)
        for q in range(PATS):
            length = jnp.sqrt(jnp.sum(lengths[q], axis=1, keepdims=True))
            total = total + (CLIP / jnp.maximum(length, CLIP)) * pat_slots[q]
        gathered[core, s] = total.astype(BF16)
        wait_blocks(pat_slots.at[pl.ds(0, PATS - 1)], pat_send)


    def forward(slot):
        for dy in (2, 1, 3):
            pltpu.make_async_remote_copy(
                gathered.at[core, slot], gathered.at[core, slot], tall_send.at[dy], tall_recv.at[dy],
                device_id=peer(dy, 0), device_id_type=MESH,
            ).start()

    @pl.when(s < OWNERS)
    def _():
        for dz in (4, 3, 5, 2, 6, 1, 7):
            pltpu.make_async_remote_copy(
                gathered.at[core, s], gathered.at[core, s], deep_send.at[dz], deep_recv.at[dz],
                device_id=peer(0, dz), device_id_type=MESH,
            ).start()
        forward(s)

    for dz in (1, 7, 2, 6, 3, 5, 4):
        slot = y * DEEP + lax.rem(z + DEEP - dz, DEEP)

        @pl.when(slot < OWNERS)
        def _():
            wait_blocks(gathered.at[core, slot], deep_recv.at[dz])
            forward(slot)

    def wait_row(owner, sem):
        @pl.when(owner < TALL - 1)
        def _():
            wait_blocks(gathered.at[0, 0:DEEP], sem)

        @pl.when(owner == TALL - 1)
        def _():
            wait_blocks(gathered.at[0, 0 : OWNERS - DEEP * (TALL - 1)], sem)

    def hand_over(dy):
        row = lax.rem(y + TALL - dy, TALL)
        blocks = gathered.at[core, pl.ds(row * DEEP, DEEP)]
        copy = pltpu.make_async_remote_copy(
            blocks, blocks, core_send.at[dy], core_recv.at[dy],
            device_id=(p + 1 - 2 * core, s), device_id_type=MESH,
        )
        copy.start()
        return copy

    rows = [hand_over(0)]
    for dy in (1, 3, 2):
        wait_row(lax.rem(y + TALL - dy, TALL), tall_recv.at[dy])
        rows.append(hand_over(dy))

    def assemble(k):
        for a in range(3):
            for t in range(LANE_TILES):
                block = gathered[k, a * LANE_TILES + t].astype(F32)
                start = a * ROWS + t % 4 * 128
                if t < 4:
                    out_ref[k, 0:32, start : start + 128] = block
                elif t < 8:
                    out_ref[k, 32:C, start : start + 128] = block
                else:
                    out_ref[k, 0:32, start + 512 : start + ROWS] = block[:, :C]
                    out_ref[k, 32:C, start + 512 : start + ROWS] = block[:, C:]

    assemble(core)
    for copy in rows:
        copy.wait()
    assemble(1 - core)

    @pl.when(s < OWNERS)
    def _():
        for dz in range(1, DEEP):
            wait_blocks(gathered.at[0, 0], deep_send.at[dz])

    for dy in range(1, TALL):
        wait_row(y, tall_send.at[dy])
    for wait in pending:
        wait()


def clipped_gradients(features, cotangent, weights, tree_noise):
    wide = WIDE * CELLS
    vmem, dma = pltpu.VMEM, pltpu.SemaphoreType.DMA
    return pl.pallas_call(
        kernel,
        out_shape=[jax.ShapeDtypeStruct((2, C, 3 * ROWS), F32)] * 2,
        in_specs=[pl.BlockSpec(memory_space=pltpu.HBM)] * 4,
        out_specs=[pl.BlockSpec(memory_space=vmem)] * 2,
        scratch_shapes=[
            vmem((PLANES, C, CELLS), BF16),
            vmem((PLANES, C, CELLS), BF16),
            vmem((2, C, 3 * ROWS), F32),
            vmem((2, C, 3 * ROWS), F32),
            vmem((C, wide), BF16),
            vmem((TAPS, 16, CELLS), BF16),
            vmem((2, 3 * C, ROWS), BF16),
            vmem((3 * C, ROWS), BF16),
            vmem((PADDED, wide), BF16),
            vmem((PADDED, wide), BF16),
            vmem((ROWS, wide), BF16),
            vmem((3 * C, wide), F32),
            vmem((C, wide), F32),
            vmem((C, wide), F32),
            vmem((C, wide), F32),
            vmem((3 * C, wide), BF16),
            vmem((3 * C, PADDED), F32),
            vmem((2, C, CELLS), BF16),
            vmem((2, C, CELLS), BF16),
            vmem((2, 2, C, CELLS), BF16),
            vmem((ROWS, 4 * CELLS), BF16),
            vmem((3 * C, 4 * CELLS), F32),
            vmem((C, 2 * CELLS), F32),
            vmem((C, wide), F32),
            vmem((5, 1, 128), F32),
            vmem((5, SLABS, 1, 128), F32),
            vmem((2, OWNERS) + BLOCK, BF16),
            vmem((2, SLABS) + BLOCK, BF16),
            vmem((2,) + BLOCK, F32),
            vmem((PATS,) + BLOCK, F32),
            vmem((2, SLABS) + BLOCK, BF16),
            vmem((PATS, 1, 128), F32),
            dma((3, 2)), dma((3, 2)), dma((5,)), dma((5,)), dma((2,)), dma((2,)), dma, dma, dma, dma, dma((DEEP,)), dma((DEEP,)), dma((TALL,)), dma((TALL,)), dma((TALL,)), dma((TALL,)), dma((4,)),
        ],
        compiler_params=pltpu.CompilerParams(
            collective_id=0, has_side_effects=True, vmem_limit_bytes=32 * 1024 * 1024
        ),
    )(features, cotangent, weights, tree_noise)


def per_device(features, cotangent, weights, prev_state, tree_noise):
    planes = (features[0].transpose(1, 0, 2), cotangent[0].transpose(1, 0, 2), weights, tree_noise)
    total, stepped = clipped_gradients(*(pltpu.with_memory_space_constraint(v, pltpu.HBM) for v in planes))
    return prev_state + total, stepped - RATE * total


def solution(mesh):
    return jax.shard_map(
        per_device,
        mesh=mesh,
        in_specs=(P("pat", None, "slab", None), P("pat", None, "slab", None), P(), P(), P()),
        out_specs=(P(), P()),
        check_vma=False,
    )
```

```python
import jax
import jax.numpy as jnp
from jax import lax
from jax.experimental import pallas as pl
from jax.experimental.pallas import tpu as pltpu
from jax.sharding import PartitionSpec as P

MESH = pl.DeviceIdType.MESH
C = 64
W = 24
CELLS = 384
PLANES = 6
WIDE = PLANES + 2
TAPS = 9
ROWS = TAPS * C
PADDED = 640
DEEP = 8
TALL = 4
SLABS = TALL * DEEP
PATS = 8
OWNERS = 27
LANE_TILES = 9
BLOCK = (32, 128)
EPS = 1e-05
CLIP = 400.0
RATE = 0.1
COUNT = SLABS * PLANES * CELLS
F32 = jnp.float32
BF16 = jnp.bfloat16


def far_first():
    steps = [(dy, dz) for dy in range(TALL) for dz in range(DEEP) if dy or dz]
    return sorted(steps, key=lambda d: -min(d[0], TALL - d[0]) - min(d[1], DEEP - d[1]))


def sigmoid(v):
    return 1.0 / (1.0 + jnp.exp(-v))


def plane(j, count=1):
    return slice(j * CELLS, (j + count) * CELLS)


def kernel(
    feat_hbm, cot_hbm, w_hbm, noise_hbm, out_ref, stepped_ref,
    feat_ref, cot_ref, w_ref, noise_ref,
    cot, masks, kst, kback, im_feat, im_hid, im_cot, parts, normed_one, normed_two, grad,
    lhs, acc, feat_halo, cot_halo, feat_far, im_far, far_parts, outer_first, slope_one, rows_out, slots, kg, reduced, scaled, pat_slots, gathered, lengths,
    halo_send, halo_recv, row_send, row_recv, red_send, red_recv, pat_send, pat_recv, len_send, len_recv, deep_send, deep_recv, tall_send, tall_recv, core_send, core_recv, load_sem,
):
    p = lax.axis_index("pat")
    s = lax.axis_index("slab")
    core = lax.rem(p, 2)
    y, z = lax.div(s, DEEP), lax.rem(s, DEEP)

    def peer(dy, dz):
        return (p, lax.rem(y + dy, TALL) * DEEP + lax.rem(z + dz, DEEP))

    slab_peers = [peer(dy, dz) for dy, dz in far_first()]

    def slab_peer(k):
        return (p, lax.rem(s + k, SLABS))

    def pat_peer(k):
        return (lax.rem(p + k, PATS), s)

    pending = []
    barrier = pltpu.get_barrier_semaphore()

    for other in slab_peers:
        pl.semaphore_signal(barrier, inc=1, device_id=other, device_id_type=MESH)

    @pl.loop(1, PATS)
    def _(k):
        pl.semaphore_signal(barrier, inc=1, device_id=pat_peer(k), device_id_type=MESH)

    loads = [
        pltpu.make_async_copy(source, target, load_sem.at[i])
        for i, (source, target) in enumerate(((feat_hbm, feat_ref), (w_hbm, w_ref), (cot_hbm, cot_ref), (noise_hbm, noise_ref)))
    ]
    for load in loads[:2]:
        load.start()

    def halo_copies(stage, low, high, landing):
        return (
            pltpu.make_async_remote_copy(
                low, landing.at[1], halo_send.at[stage, 0], halo_recv.at[stage, 1],
                device_id=slab_peer(SLABS - 1), device_id_type=MESH,
            ),
            pltpu.make_async_remote_copy(
                high, landing.at[0], halo_send.at[stage, 1], halo_recv.at[stage, 0],
                device_id=slab_peer(1), device_id_type=MESH,
            ),
        )

    def wait_blocks(ref, sem):
        pltpu.make_async_copy(ref, ref, sem).wait()

    def wait_owned(ref, sem):
        @pl.when(s < OWNERS)
        def _():
            wait_blocks(ref.at[pl.ds(0, OWNERS - 1)], sem)

        @pl.when(s >= OWNERS)
        def _():
            wait_blocks(ref.at[pl.ds(0, OWNERS)], sem)

    def wait_red(k):
        @pl.when(s < OWNERS)
        def _():
            wait_blocks(reduced.at[k, pl.ds(0, SLABS - 1)], red_recv.at[k])

    def kept(j):
        if 0 < j < WIDE - 1:
            return 1.0
        return jnp.where(s == (0 if j == 0 else SLABS - 1), 0.0, 1.0).astype(F32)

    def share_row(r, row):
        rows_out[r] = row

        for other in slab_peers:
            pltpu.make_async_remote_copy(
                rows_out.at[r], slots.at[r, s], row_send.at[r], row_recv.at[r],
                device_id=other, device_id_type=MESH,
            ).start()

        slots[r, s] = row
        pending.append(lambda: wait_blocks(slots.at[r, pl.ds(0, SLABS - 1)], row_send.at[r]))

    def row_total(r):
        most = slots.at[r, pl.ds(0, SLABS - 1)]
        pltpu.make_async_copy(most, most, row_recv.at[r]).wait()
        return jnp.sum(slots[r], axis=0)

    def share_pair(r, one, two):
        lanes = jnp.transpose(jnp.concatenate([one, two], axis=0))
        share_row(r, jnp.sum(lanes, axis=0, keepdims=True))

    def pair_total(r):
        row = row_total(r) * (1.0 / COUNT)
        column = jnp.transpose(jnp.broadcast_to(row, (128, 128)))[:, :1]
        return column[:C], column[C:]

    def taps(values, im, j):
        for t in range(TAPS):
            shift = (t // 3 - 1) * W + (t % 3 - 1)
            if shift == 0:
                piece = values
            else:
                piece = pltpu.roll(values, (-shift) % CELLS, 1)
                piece = (piece.reshape(C // 16, 16, CELLS) * masks[t]).reshape(C, CELLS)
            im[t * C : (t + 1) * C, plane(j)] = piece

    def multiply(matrix, im, first, count):
        parts[:, plane(first, count)] = jnp.dot(matrix, im[0:ROWS, plane(first, count)], preferred_element_type=F32)

    def combined(j):
        return (
            parts[0:C, plane(j)]
            + parts[C : 2 * C, plane(j + 1)]
            + parts[2 * C : 3 * C, plane(j + 2)]
        )

    def lane_sum(v):
        return v[:, 0:128] + v[:, 128:256] + v[:, 256:384]

    cell = lax.broadcasted_iota(jnp.int32, (16, CELLS), 1)
    row, col = lax.div(cell, W), lax.rem(cell, W)
    for t in range(TAPS):
        b, e = t // 3 - 1, t % 3 - 1
        inside = (row + b >= 0) & (row + b < CELLS // W) & (col + e >= 0) & (col + e < W)
        masks[t] = jnp.where(inside, 1.0, 0.0).astype(BF16)
    loads[1].wait()
    for a in range(3):
        kst[0, a * C : (a + 1) * C, :] = w_ref[0, :, a * ROWS : (a + 1) * ROWS].astype(BF16)
    loads[0].wait()
    for load in loads[2:]:
        load.start()
    for j in range(1, WIDE - 1):
        taps(feat_ref[j - 1], im_feat, j)
    pl.semaphore_wait(barrier, SLABS - 1 + PATS - 1)

    halos = [halo_copies(0, feat_ref.at[0], feat_ref.at[PLANES - 1], feat_halo), halo_copies(1, cot_ref.at[0], cot_ref.at[PLANES - 1], cot_halo),
        halo_copies(2, feat_ref.at[1:3], feat_ref.at[3:5], feat_far)]
    for pair in (halos[0], halos[2]):
        for copy in pair:
            copy.start()
    multiply(kst[0], im_feat, 1, PLANES)
    for copy in halos[0]:
        copy.wait_recv()
        pending.append(copy.wait_send)
    for side, j, a in ((0, 0, 0), (1, WIDE - 1, 2)):
        taps(feat_halo[side] * kept(j).astype(BF16), im_feat, j)
        parts[a * C : (a + 1) * C, plane(j)] = jnp.dot(
            kst[0, a * C : (a + 1) * C, :], im_feat[0:ROWS, plane(j)], preferred_element_type=F32
        )

    def convolved(target):
        one = two = jnp.zeros((C, 128), F32)
        for z in range(PLANES):
            value = combined(z)
            target[:, plane(z + 1)] = value
            one, two = one + lane_sum(value), two + lane_sum(value * value)
        return one, two

    share_pair(0, *convolved(normed_one))

    for k in range(2):
        for slot in range(OWNERS, SLABS):
            gathered[k, slot] = jnp.zeros(BLOCK, BF16)
    for load in loads[2:]:
        load.wait()
    stepped_ref[...] = w_ref[...] - RATE * noise_ref[...]
    for a in range(3):
        kst[1, a * C : (a + 1) * C, :] = w_ref[1, :, a * ROWS : (a + 1) * ROWS].astype(BF16)
    turned = jnp.transpose(w_ref[1].astype(BF16).astype(F32))
    for a in range(3):
        for t in range(TAPS):
            block = turned[(a * TAPS + t) * C : (a * TAPS + t + 1) * C, :]
            u = TAPS - 1 - t
            kback[(2 - a) * C : (3 - a) * C, u * C : (u + 1) * C] = block.astype(BF16)
        for j in range(WIDE):
            if not a <= j < a + PLANES:
                lhs[a * C : (a + 1) * C, plane(j)] = jnp.zeros((C, CELLS), BF16)
    for im in (im_feat, im_hid):
        im[ROWS:PADDED, :] = jnp.zeros((PADDED - ROWS, WIDE * CELLS), BF16)

    parts[C : 3 * C, plane(0)] = jnp.dot(kst[0, C : 3 * C, :], im_feat[0:ROWS, plane(0)], preferred_element_type=F32)
    parts[0 : 2 * C, plane(WIDE - 1)] = jnp.dot(
        kst[0, 0 : 2 * C, :], im_feat[0:ROWS, plane(WIDE - 1)], preferred_element_type=F32
    )
    for copy in halos[2]:
        copy.wait()
    for i in range(4):
        taps(feat_far[i // 2, i % 2], im_far, i)
    far_parts[...] = jnp.dot(kst[0], im_far[...], preferred_element_type=F32)
    low, mid, high = slice(0, C), slice(C, 2 * C), slice(2 * C, 3 * C)
    normed_one[:, plane(0)] = far_parts[low, plane(1)] + parts[mid, plane(0)] + parts[high, plane(1)]
    normed_one[:, plane(WIDE - 1)] = parts[low, plane(6)] + parts[mid, plane(7)] + far_parts[high, plane(2)]
    outer_first[:, plane(0)] = far_parts[low, plane(0)] + far_parts[mid, plane(1)] + parts[high, plane(0)]
    outer_first[:, plane(1)] = parts[low, plane(7)] + far_parts[mid, plane(2)] + far_parts[high, plane(3)]

    centre_one, squares = pair_total(0)
    for copy in halos[1]:
        copy.start()
    spread_one = lax.rsqrt(squares - centre_one * centre_one + EPS)
    for j in range(WIDE):
        value = (normed_one[:, plane(j)] - centre_one) * spread_one
        normed_one[:, plane(j)] = value
        taps((value * sigmoid(value) * kept(j)).astype(BF16), im_hid, j)
        if j % 2:
            multiply(kst[1], im_hid, j - 1, 2)

    def slope(v):
        h = sigmoid(v)
        return h * (1.0 + v * (1.0 - h))

    share_pair(1, *convolved(normed_two))
    for i, j, a in ((0, 0, low), (1, WIDE - 1, high)):
        value = (outer_first[:, plane(i)] - centre_one) * spread_one
        taps((value * sigmoid(value) * kept(j)).astype(BF16), im_far, i)
        far_parts[a, plane(i)] = jnp.dot(kst[1, a, :], im_far[:, plane(i)], preferred_element_type=F32)
    normed_two[:, plane(0)] = far_parts[low, plane(0)] + parts[mid, plane(0)] + parts[high, plane(1)]
    normed_two[:, plane(WIDE - 1)] = parts[low, plane(6)] + parts[mid, plane(7)] + far_parts[high, plane(1)]
    centre_two, squares = pair_total(1)
    spread_two = lax.rsqrt(squares - centre_two * centre_two + EPS)
    for copy in halos[1]:
        copy.wait()
    def second_gradient(j, carry, upstream=None):
        value = (normed_two[:, plane(j)] - centre_two) * spread_two
        normed_two[:, plane(j)] = value
        upstream = cot_ref[j - 1] if upstream is None else upstream
        g = upstream.astype(F32) * slope(value)
        grad[:, plane(j)] = g
        return carry[0] + lane_sum(g), carry[1] + lane_sum(g * value)

    zero = jnp.zeros((C, 128), F32)
    carry = (zero, zero)
    for j in range(1, WIDE - 1):
        carry = second_gradient(j, carry)
    one, two = carry
    share_pair(2, one, two)
    second_gradient(0, (zero, zero), cot_halo[0])
    second_gradient(WIDE - 1, (zero, zero), cot_halo[1])
    for j in range(1, WIDE - 1):
        slope_one[:, plane(j)] = slope(normed_one[:, plane(j)])
    mean_two, cross_two = pair_total(2)

    for j in range(WIDE):
        value = spread_two * (grad[:, plane(j)] - mean_two - normed_two[:, plane(j)] * cross_two)
        value = (value * kept(j)).astype(BF16)
        cot[:, plane(j)] = value
        taps(value, im_cot, j)
        if j % 2:
            multiply(kback[...], im_cot, j - 1, 2)

    def first_gradient(j, carry):
        value = normed_one[:, plane(j + 1)]
        g = combined(j) * slope_one[:, plane(j + 1)]
        grad[:, plane(j + 1)] = g
        return carry[0] + lane_sum(g), carry[1] + lane_sum(g * value)

    carry = (zero, zero)
    for j in range(PLANES):
        carry = first_gradient(j, carry)
    one, two = carry
    share_pair(3, one, two)

    def kernel_gradient(k, im):
        def send(first, count):
            for a in range(3):
                for t in range(first, first + count):
                    owner = a * LANE_TILES + t

                    @pl.when(s != owner)
                    def _():
                        pltpu.make_async_remote_copy(
                            kg.at[k, owner], reduced.at[k, s], red_send.at[k], red_recv.at[k],
                            device_id=(p, owner), device_id_type=MESH,
                        ).start()

        for first in (0, 256, 512):
            width = 256 if first < 512 else 128
            term = lax.dot_general(
                lhs[...], im[first : first + width, :], (((1,), (1,)), ((), ())), preferred_element_type=F32
            )
            for a in range(3):
                low, high = term[a * C : a * C + 32], term[a * C + 32 : (a + 1) * C]
                if first < 512:
                    for t in range(2):
                        lanes = slice(t * 128, (t + 1) * 128)
                        kg[k, a * LANE_TILES + first // 128 + t] = low[:, lanes].astype(BF16)
                        kg[k, a * LANE_TILES + 4 + first // 128 + t] = high[:, lanes].astype(BF16)
                else:
                    kg[k, a * LANE_TILES + 8] = (low + pltpu.roll(high, C, 1)).astype(BF16)
            if first < 512:
                send(first // 128, 2)
                send(4 + first // 128, 2)
            else:
                send(8, 1)

        @pl.when(s < OWNERS)
        def _():
            reduced[k, s] = kg[k, s]

        pending.append(lambda: wait_owned(kg.at[k], red_send.at[k]))

    def place(j, value):
        for a in range(3):
            lhs[a * C : (a + 1) * C, plane(j + a)] = value

    for j in range(PLANES):
        place(j, cot[:, plane(j + 1)])

    kernel_gradient(1, im_hid)
    mean_one, cross_one = pair_total(3)

    for j in range(PLANES):
        value = spread_one * (grad[:, plane(j + 1)] - mean_one - normed_one[:, plane(j + 1)] * cross_one)
        place(j, value.astype(BF16))

    kernel_gradient(0, im_feat)

    @pl.when(s < OWNERS)
    def _():
        for k in (1, 0):
            wait_red(k)
            scaled[k] = jnp.sum(reduced[k].astype(F32), axis=0)

    @pl.when(s >= OWNERS)
    def _():
        for k in (0, 1):
            scaled[k] = jnp.zeros(BLOCK, F32)

    squared = jnp.sum(scaled[0] * scaled[0] + scaled[1] * scaled[1], axis=0, keepdims=True)
    share_row(4, squared)

    @pl.when(s < OWNERS)
    def _():
        @pl.loop(1, PATS)
        def _(q):
            peer = lax.rem(p + q, PATS)
            pltpu.make_async_remote_copy(
                scaled.at[lax.rem(peer, 2)], pat_slots.at[p], pat_send, pat_recv,
                device_id=(peer, s), device_id_type=MESH,
            ).start()

        pat_slots[p] = scaled[core]

    lengths[p] = row_total(4)

    @pl.when(s < OWNERS)
    def _():
        @pl.loop(1, PATS)
        def _(q):
            pltpu.make_async_remote_copy(
                lengths.at[p], lengths.at[p], len_send, len_recv, device_id=pat_peer(q), device_id_type=MESH
            ).start()

        wait_blocks(pat_slots.at[pl.ds(0, PATS - 1)], pat_recv)
        wait_blocks(lengths.at[pl.ds(0, PATS - 1)], len_recv)
        wait_blocks(lengths.at[pl.ds(0, PATS - 1)], len_send)
        total = jnp.zeros(BLOCK, F32)
        for q in range(PATS):
            length = jnp.sqrt(jnp.sum(lengths[q], axis=1, keepdims=True))
            total = total + (CLIP / jnp.maximum(length, CLIP)) * pat_slots[q]
        gathered[core, s] = total.astype(BF16)
        wait_blocks(pat_slots.at[pl.ds(0, PATS - 1)], pat_send)


    def forward(slot):
        for dy in (2, 1, 3):
            pltpu.make_async_remote_copy(
                gathered.at[core, slot], gathered.at[core, slot], tall_send.at[dy], tall_recv.at[dy],
                device_id=peer(dy, 0), device_id_type=MESH,
            ).start()

    @pl.when(s < OWNERS)
    def _():
        for dz in (4, 3, 5, 2, 6, 1, 7):
            pltpu.make_async_remote_copy(
                gathered.at[core, s], gathered.at[core, s], deep_send.at[dz], deep_recv.at[dz],
                device_id=peer(0, dz), device_id_type=MESH,
            ).start()
        forward(s)

    for dz in (1, 7, 2, 6, 3, 5, 4):
        slot = y * DEEP + lax.rem(z + DEEP - dz, DEEP)

        @pl.when(slot < OWNERS)
        def _():
            wait_blocks(gathered.at[core, slot], deep_recv.at[dz])
            forward(slot)

    def wait_row(owner, sem):
        @pl.when(owner < TALL - 1)
        def _():
            wait_blocks(gathered.at[0, 0:DEEP], sem)

        @pl.when(owner == TALL - 1)
        def _():
            wait_blocks(gathered.at[0, 0 : OWNERS - DEEP * (TALL - 1)], sem)

    def hand_over(dy):
        row = lax.rem(y + TALL - dy, TALL)
        blocks = gathered.at[core, pl.ds(row * DEEP, DEEP)]
        copy = pltpu.make_async_remote_copy(
            blocks, blocks, core_send.at[dy], core_recv.at[dy],
            device_id=(p + 1 - 2 * core, s), device_id_type=MESH,
        )
        copy.start()
        return copy

    rows = [hand_over(0)]
    for dy in (1, 3, 2):
        wait_row(lax.rem(y + TALL - dy, TALL), tall_recv.at[dy])
        rows.append(hand_over(dy))

    def assemble(k):
        for a in range(3):
            for t in range(LANE_TILES):
                block = gathered[k, a * LANE_TILES + t].astype(F32)
                start = a * ROWS + t % 4 * 128
                if t < 4:
                    out_ref[k, 0:32, start : start + 128] = block
                elif t < 8:
                    out_ref[k, 32:C, start : start + 128] = block
                else:
                    out_ref[k, 0:32, start + 512 : start + ROWS] = block[:, :C]
                    out_ref[k, 32:C, start + 512 : start + ROWS] = block[:, C:]

    assemble(core)
    for copy in rows:
        copy.wait()
    assemble(1 - core)

    @pl.when(s < OWNERS)
    def _():
        for dz in range(1, DEEP):
            wait_blocks(gathered.at[0, 0], deep_send.at[dz])

    for dy in range(1, TALL):
        wait_row(y, tall_send.at[dy])
    for wait in pending:
        wait()


def clipped_gradients(features, cotangent, weights, tree_noise):
    wide = WIDE * CELLS
    vmem, dma = pltpu.VMEM, pltpu.SemaphoreType.DMA
    return pl.pallas_call(
        kernel,
        out_shape=[jax.ShapeDtypeStruct((2, C, 3 * ROWS), F32)] * 2,
        in_specs=[pl.BlockSpec(memory_space=pltpu.HBM)] * 4,
        out_specs=[pl.BlockSpec(memory_space=vmem)] * 2,
        scratch_shapes=[
            vmem((PLANES, C, CELLS), BF16),
            vmem((PLANES, C, CELLS), BF16),
            vmem((2, C, 3 * ROWS), F32),
            vmem((2, C, 3 * ROWS), F32),
            vmem((C, wide), BF16),
            vmem((TAPS, 16, CELLS), BF16),
            vmem((2, 3 * C, ROWS), BF16),
            vmem((3 * C, ROWS), BF16),
            vmem((PADDED, wide), BF16),
            vmem((PADDED, wide), BF16),
            vmem((ROWS, wide), BF16),
            vmem((3 * C, wide), F32),
            vmem((C, wide), F32),
            vmem((C, wide), F32),
            vmem((C, wide), F32),
            vmem((3 * C, wide), BF16),
            vmem((3 * C, PADDED), F32),
            vmem((2, C, CELLS), BF16),
            vmem((2, C, CELLS), BF16),
            vmem((2, 2, C, CELLS), BF16),
            vmem((ROWS, 4 * CELLS), BF16),
            vmem((3 * C, 4 * CELLS), F32),
            vmem((C, 2 * CELLS), F32),
            vmem((C, wide), F32),
            vmem((5, 1, 128), F32),
            vmem((5, SLABS, 1, 128), F32),
            vmem((2, OWNERS) + BLOCK, BF16),
            vmem((2, SLABS) + BLOCK, BF16),
            vmem((2,) + BLOCK, F32),
            vmem((PATS,) + BLOCK, F32),
            vmem((2, SLABS) + BLOCK, BF16),
            vmem((PATS, 1, 128), F32),
            dma((3, 2)), dma((3, 2)), dma((5,)), dma((5,)), dma((2,)), dma((2,)), dma, dma, dma, dma, dma((DEEP,)), dma((DEEP,)), dma((TALL,)), dma((TALL,)), dma((TALL,)), dma((TALL,)), dma((4,)),
        ],
        compiler_params=pltpu.CompilerParams(
            collective_id=0, has_side_effects=True, vmem_limit_bytes=32 * 1024 * 1024
        ),
    )(features, cotangent, weights, tree_noise)


def per_device(features, cotangent, weights, prev_state, tree_noise):
    planes = (features[0].transpose(1, 0, 2), cotangent[0].transpose(1, 0, 2), weights, tree_noise)
    total, stepped = clipped_gradients(*(pltpu.with_memory_space_constraint(v, pltpu.HBM) for v in planes))
    return prev_state + total, stepped - RATE * total


def solution(mesh):
    return jax.shard_map(
        per_device,
        mesh=mesh,
        in_specs=(P("pat", None, "slab", None), P("pat", None, "slab", None), P(), P(), P()),
        out_specs=(P(), P()),
        check_vma=False,
    )
```
